32 devices in a mesh: dp: 16 (over z, y, core), fsdp: 2 (over x).
Axes of the slice: x: 2, y: 2, z: 4, core: 2. Of those that a mesh axis runs over, the one named last changes fastest.
Arguments:
- acts: bfloat16 [4096, 2048], P(('dp', 'fsdp')), may hold values from -6 to 6
- grad_out: bfloat16 [4096, 2048], P(('dp', 'fsdp')), may hold values from -60 to 60
- weight: bfloat16 [2048, 2048], P('fsdp'), may hold values from -0.125 to 0.125
- basis: bfloat16 [2048, 512], P('fsdp'), may hold values from -3 to 3
- first_moment: float32 [512, 2048], P(('dp', 'fsdp')), may hold values from -4 to 4
- second_moment: float32 [512, 2048], P(('dp', 'fsdp')), may hold values from 0.0001 to 0.01
Outputs:
- grad_in: bfloat16 [4096, 2048], P(('dp', 'fsdp'))
- first_new: float32 [512, 2048], P(('dp', 'fsdp'))
- second_new: float32 [512, 2048], P(('dp', 'fsdp'))
- weight_update: bfloat16 [2048, 2048], P('fsdp')
The draws below stay inside these ranges and needn't reach their ends.
All inputs are finite; a program needn't handle non-finite values.
Results may differ from the reference program's by a relative error of at most 0.0056.
Values may be sent and summed in bfloat16 or wider, within the bound.
A program may use at most 64 MiB of HBM per device.

```python
import math
import jax
import jax.numpy as jnp

D_IN = 2048
D_OUT = 2048
RANK = 512
TOKENS = 4096


def draw_grad_out(key, part):
    key = jax.random.fold_in(key, 11)
    noise_key, scale_key = jax.random.split(key, 2)
    column_scale = jnp.exp(jax.random.uniform(scale_key, (D_OUT,), jnp.float32, 0.0, math.log(10.0)))
    noise = jnp.clip(jax.random.normal(noise_key, (TOKENS, D_OUT), jnp.float32), -6.0, 6.0)
    values = noise * column_scale[None, :]
    return values.astype(jnp.bfloat16)


def draw_basis(key, part):
    key = jax.random.fold_in(key, 23)
    noise_key, scale_key = jax.random.split(key, 2)
    ladder = jnp.exp(jnp.arange(RANK, dtype=jnp.float32) * (math.log(10.0) / max(RANK - 1, 1)))
    jitter = jnp.exp(jax.random.uniform(scale_key, (RANK,), jnp.float32, 0.0, math.log(2.0)))
    column_scale = ladder * jitter / math.sqrt(D_IN)
    noise = jnp.clip(jax.random.normal(noise_key, (D_IN, RANK), jnp.float32), -5.0, 5.0)
    return (noise * column_scale[None, :]).astype(jnp.bfloat16)


def levels(rng, shape, cuts, least, largest):
    loudness, own = 1.0, jax.random.fold_in(rng, 6)
    for axis_at, parts in cuts:
        heights = jnp.exp(jax.random.uniform(jax.random.fold_in(own, axis_at), (parts,), jnp.float32, least / len(cuts), largest / len(cuts)))
        loudness = loudness * jnp.repeat(heights, shape[axis_at] // parts).reshape([-1 if axis == axis_at else 1 for axis in range(len(shape))])
    return loudness


def normal_values(stream_key, shape, scale, reach, cuts=(), kind=jnp.bfloat16):
    level = levels(stream_key, shape, cuts, -0.22, 0.18) if cuts else 1.0
    result = jax.random.normal(stream_key, shape, jnp.float32) * scale * level
    return jnp.minimum(jnp.maximum(result, -reach), reach).astype(kind)


def setup_inputs(seed: int = 0) -> dict:
    arg_keys = jax.random.split(jax.random.key(seed), 7)
    acts = normal_values(arg_keys[0], (TOKENS, D_IN), 1.0, 6.0, ((0, 32),))
    grad_out = draw_grad_out(jax.random.fold_in(arg_keys[6], 71), 0)
    weight = normal_values(arg_keys[2], (D_IN, D_OUT), D_IN ** -0.5, 0.125, ((0, 2),))
    basis = draw_basis(jax.random.fold_in(arg_keys[6], 71), 0)
    first_moment = normal_values(arg_keys[4], (RANK, D_OUT), 0.3, 4.0, ((0, 32),), jnp.float32)
    second_moment = jnp.clip(jnp.exp(math.log(0.01) - 4.6051702 * jax.random.uniform(arg_keys[5], (RANK, D_OUT), jnp.float32) ** levels(arg_keys[5], (RANK, D_OUT), ((0, 32),), -0.2, 0.2)), 0.0001, 0.01)
    return dict(acts=acts, grad_out=grad_out, weight=weight, basis=basis, first_moment=first_moment, second_moment=second_moment)


first_bias = 1.0 - 0.9 ** 10
second_bias = 1.0 - 0.999 ** 10

def reference(acts, grad_out, weight, basis, first_moment, second_moment):
    grad_in = jnp.dot(grad_out, weight.T, preferred_element_type=jnp.float32).astype(jnp.bfloat16)
    coords = jnp.dot(acts, basis, preferred_element_type=jnp.float32).astype(jnp.bfloat16)
    projected = jnp.dot(coords.T, grad_out, preferred_element_type=jnp.float32)
    total = jnp.sum(projected * projected)
    limit = math.sqrt(RANK * D_OUT)
    factor = jnp.minimum(1.0, limit / (jnp.sqrt(total) + 1e-06))
    clipped = factor * projected
    first_new = 0.9 * first_moment + 0.1 * clipped
    second_new = 0.999 * second_moment + 0.001 * clipped * clipped
    direction = (first_new / first_bias / (jnp.sqrt(second_new / second_bias) + 1e-08)).astype(jnp.bfloat16)
    update = jnp.dot(basis, direction, preferred_element_type=jnp.float32)
    weight_update = (0.25 * update).astype(jnp.bfloat16)
    return (grad_in, first_new, second_new, weight_update)
```

```python
import functools
import math

import jax
import jax.numpy as jnp
from jax import lax
from jax.experimental import pallas as pl
from jax.experimental.pallas import tpu as pltpu
from jax.sharding import PartitionSpec as P

MESH = pl.DeviceIdType.MESH
F32 = jnp.float32
BF16 = jnp.bfloat16

first_bias = 1.0 - 0.9**10
second_bias = 1.0 - 0.999**10

PLANES = 8
CHUNKS = 4


def clipped_adam(projected, total, first_moment, second_moment, entries):
    limit = math.sqrt(entries)
    factor = jnp.minimum(1.0, limit / (jnp.sqrt(total) + 1e-06))
    clipped = factor * projected
    first_new = 0.9 * first_moment + 0.1 * clipped
    second_new = 0.999 * second_moment + 0.001 * clipped * clipped
    direction = first_new / first_bias / (jnp.sqrt(second_new / second_bias) + 1e-08)
    return first_new, second_new, direction.astype(BF16)


def step_kernel(
    acts_ref, grad_ref, weight_hbm, basis_ref, first_ref, second_ref,
    grad_in_ref, first_out, second_out, gathered_hbm,
    weight, acts_pair, basis_perm, partial, partial_in, grads, coords,
    own, mine16, arrived, sums_out, sums_in, gathered, back_out, back_in,
    weight_sem, out_sem,
    acts_s, acts_r, coords_s, coords_r, gx_s, gx_r, gc_s, gc_r, gf_s, gf_r,
    rs_s, rs_r, sum_s, sum_r, back_s, back_r,
    az_s, az_r, ax_s, ax_r, ac_s, ac_r, af_s, af_r,
):
    dp = lax.axis_index("dp")
    x = lax.axis_index("fsdp")
    ox = 1 - x
    plane = dp // 2
    core = dp % 2
    oc = 1 - core
    me = core * 2 + x
    tokens, d_in = acts_ref.shape
    half = d_in // 2
    d_out = grad_ref.shape[1]
    wide = d_out // CHUNKS
    rank = basis_ref.shape[1]
    quarter = rank // 4
    rows = rank // (4 * PLANES)

    def device(p, c, f):
        return {"dp": p * 2 + c, "fsdp": f}

    partner = device(plane, core, ox)
    sibling = device(plane, oc, x)
    diagonal = device(plane, oc, ox)
    planes = [device((plane + k) % PLANES, core, x) for k in range(PLANES)]
    group = [partner, sibling, diagonal]

    def send(src, dst, s, r, to):
        copy = pltpu.make_async_remote_copy(
            src_ref=src, dst_ref=dst, send_sem=s, recv_sem=r, device_id=to, device_id_type=MESH
        )
        copy.start()
        return copy

    load = pltpu.make_async_copy(weight_hbm, weight, weight_sem)
    load.start()
    barrier = pltpu.get_barrier_semaphore()
    for to in group + planes[1:]:
        pl.semaphore_signal(barrier, inc=1, device_id=to, device_id_type=MESH)
    pl.semaphore_wait(barrier, 2 + PLANES)

    pending = []
    acts_copy = send(
        acts_ref.at[:, pl.ds(pl.multiple_of(ox * half, half), half)],
        acts_pair.at[x], acts_s, acts_r, partner,
    )
    to_partner = []
    to_sibling = []
    for n in range(CHUNKS):
        cols = pl.ds(n * wide, wide)
        to_partner.append(
            send(grad_ref.at[:, cols], grads.at[me, :, cols], gx_s.at[n], gx_r.at[n], partner)
        )
        to_sibling.append(
            send(grad_ref.at[:, cols], grads.at[me, :, cols], gc_s.at[n], gc_r.at[n], sibling)
        )
    grads[me] = grad_ref[...]

    at = lax.broadcasted_iota(jnp.int32, (rank, rank), 0)
    to = lax.broadcasted_iota(jnp.int32, (rank, rank), 1)
    source = ((to % quarter) // rows * 4 + to // quarter) * rows + to % rows
    shuffle = jnp.where(at == source, 1.0, 0.0).astype(BF16)
    basis_perm[...] = jnp.dot(basis_ref[...], shuffle, preferred_element_type=F32).astype(BF16)

    def project(block):
        return jnp.dot(block, basis_perm[...], preferred_element_type=F32)

    values = project(acts_ref[:, pl.ds(pl.multiple_of(x * half, half), half)])
    for q in range(4):
        partial[q, x] = values[:, q * quarter:(q + 1) * quarter]
    acts_copy.wait_recv()
    values = project(acts_pair[ox])
    for q in range(4):
        partial[q, ox] = values[:, q * quarter:(q + 1) * quarter]
    coord_copies = []
    for k, (to_dev, q) in enumerate(
        [(partner, core * 2 + ox), (diagonal, oc * 2 + ox), (sibling, oc * 2 + x)]
    ):
        coord_copies.append(
            send(partial.at[q], partial_in.at[k], coords_s.at[k], coords_r.at[k], to_dev)
        )
    for copy in coord_copies:
        copy.wait_recv()
    coords[core] = (partial[me] + partial_in[0]).astype(BF16)
    coords[oc] = (partial_in[1] + partial_in[2]).astype(BF16)

    scatter = []
    forward = []
    for n in range(CHUNKS):
        cols = pl.ds(n * wide, wide)
        to_partner[n].wait_recv()
        theirs = core * 2 + ox
        forward.append(
            send(grads.at[theirs, :, cols], grads.at[theirs, :, cols], gf_s.at[n], gf_r.at[n], sibling)
        )
        to_sibling[n].wait_recv()
        forward[n].wait_recv()
        chunk = lax.dot_general(
            coords[...].reshape(4 * tokens, quarter),
            grads[:, :, cols].reshape(4 * tokens, wide),
            (((0,), (0,)), ((), ())),
            preferred_element_type=F32,
        )
        chunk = chunk.reshape(PLANES, rows, wide)
        own[:, :, cols] = chunk
        mine16[:, :, cols] = chunk.astype(BF16)
        for k in range(1, PLANES):
            scatter.append(
                send(
                    mine16.at[(plane + k) % PLANES, :, cols], arrived.at[k - 1, :, cols],
                    rs_s.at[n, k - 1], rs_r.at[n, k - 1], planes[k],
                )
            )

    load.wait()

    def input_gradient(block):
        return lax.dot_general(
            block, weight[...], (((1,), (1,)), ((), ())), preferred_element_type=F32
        ).astype(BF16)

    back_out[...] = input_gradient(grads[core * 2 + ox])
    back = send(back_out, back_in, back_s, back_r, partner)
    grad_in_ref[:, pl.ds(pl.multiple_of(x * half, half), half)] = input_gradient(grad_ref[...])

    for copy in scatter:
        copy.wait_recv()
    projected = own[plane]
    for k in range(PLANES - 1):
        projected = projected + arrived[k].astype(F32)

    sums_out[0] = jnp.full((8, 128), jnp.sum(projected * projected), F32)
    copies = []
    for k in range(1, PLANES):
        copies.append(
            send(sums_out.at[0], sums_in.at[k - 1], sum_s.at[k - 1], sum_r.at[k - 1], planes[k])
        )
    total = sums_out[0]
    for k in range(PLANES - 1):
        copies[k].wait_recv()
        total = total + sums_in[k]
    sums_out[1] = total
    for k, to_dev in enumerate(group):
        j = PLANES - 1 + k
        copies.append(send(sums_out.at[1], sums_in.at[j], sum_s.at[j], sum_r.at[j], to_dev))
    for k in range(3):
        copies[PLANES - 1 + k].wait_recv()
        total = total + sums_in[PLANES - 1 + k]
    pending += copies

    first_new, second_new, direction = clipped_adam(
        projected, total[0:1, 0:1], first_ref[...], second_ref[...], rank * d_out
    )
    gathered[plane, me] = direction
    across = []
    for k in range(1, PLANES):
        block = gathered.at[plane, me]
        across.append(send(block, block, az_s.at[k - 1], az_r.at[k - 1], planes[k]))
    first_out[...] = first_new
    second_out[...] = second_new
    along = []
    siblings = []
    theirs = core * 2 + ox

    def relay(k):
        at_plane = (plane + PLANES - k) % PLANES
        along[k].wait_recv()
        block = gathered.at[at_plane, theirs]
        siblings.append(send(block, block, af_s.at[k], af_r.at[k], sibling))

    for k in range(PLANES):
        if k:
            across[k - 1].wait_recv()
        at_plane = (plane + PLANES - k) % PLANES
        block = gathered.at[at_plane, me]
        along.append(send(block, block, ax_s.at[k], ax_r.at[k], partner))
        siblings.append(send(block, block, ac_s.at[k], ac_r.at[k], sibling))
        if k:
            relay(k - 1)
    relay(PLANES - 1)
    back.wait_recv()
    grad_in_ref[:, pl.ds(pl.multiple_of(ox * half, half), half)] = back_in[...]
    for copy in siblings:
        copy.wait_recv()
    store = pltpu.make_async_copy(gathered, gathered_hbm, out_sem)
    store.start()
    pending += [acts_copy, back] + to_partner + to_sibling + coord_copies + forward
    pending += scatter + across + along + siblings
    for copy in pending:
        copy.wait_send()
    store.wait()


def update_kernel(basis_ref, direction_ref, out_ref):
    update = jnp.dot(basis_ref[...], direction_ref[...], preferred_element_type=F32)
    out_ref[...] = (0.25 * update).astype(BF16)


def on_device_kernel(acts, grad_out, weight, basis, first_moment, second_moment):
    tokens, d_in = acts.shape
    d_out = grad_out.shape[1]
    half = d_in // 2
    rank = basis.shape[1]
    quarter = rank // 4
    rows = rank // (4 * PLANES)
    vmem = pl.BlockSpec(memory_space=pltpu.VMEM)
    anywhere = pl.BlockSpec(memory_space=pl.ANY)
    dma = pltpu.SemaphoreType.DMA
    grad_in, first_new, second_new, direction = pl.pallas_call(
        step_kernel,
        out_shape=(
            jax.ShapeDtypeStruct((tokens, d_in), BF16),
            jax.ShapeDtypeStruct(first_moment.shape, F32),
            jax.ShapeDtypeStruct(second_moment.shape, F32),
            jax.ShapeDtypeStruct((PLANES, 4, rows, d_out), BF16),
        ),
        in_specs=[vmem, vmem, anywhere, vmem, vmem, vmem],
        out_specs=(vmem, vmem, vmem, anywhere),
        scratch_shapes=[
            pltpu.VMEM(weight.shape, BF16),
            pltpu.VMEM((2, tokens, half), BF16),
            pltpu.VMEM(basis.shape, BF16),
            pltpu.VMEM((4, 2, tokens, quarter), F32),
            pltpu.VMEM((3, 2, tokens, quarter), F32),
            pltpu.VMEM((4, tokens, d_out), BF16),
            pltpu.VMEM((2, 2, tokens, quarter), BF16),
            pltpu.VMEM((PLANES, rows, d_out), F32),
            pltpu.VMEM((PLANES, rows, d_out), BF16),
            pltpu.VMEM((PLANES - 1, rows, d_out), BF16),
            pltpu.VMEM((2, 8, 128), F32),
            pltpu.VMEM((PLANES + 2, 8, 128), F32),
            pltpu.VMEM((PLANES, 4, rows, d_out), BF16),
            pltpu.VMEM((tokens, half), BF16),
            pltpu.VMEM((tokens, half), BF16),
            dma, dma,
            dma, dma, dma((3,)), dma((3,)),
            dma((CHUNKS,)), dma((CHUNKS,)), dma((CHUNKS,)), dma((CHUNKS,)),
            dma((CHUNKS,)), dma((CHUNKS,)),
            dma((CHUNKS, PLANES - 1)), dma((CHUNKS, PLANES - 1)),
            dma((PLANES + 2,)), dma((PLANES + 2,)), dma, dma,
            dma((PLANES - 1,)), dma((PLANES - 1,)),
            dma((PLANES,)), dma((PLANES,)), dma((PLANES,)), dma((PLANES,)),
            dma((PLANES,)), dma((PLANES,)),
        ],
        compiler_params=pltpu.CompilerParams(
            collective_id=0, has_side_effects=True, vmem_limit_bytes=48 * 1024 * 1024
        ),
        name="galore_step",
    )(acts, grad_out, weight, basis, first_moment, second_moment)
    direction = direction.reshape(rank, d_out)
    wide = 512
    weight_update = pl.pallas_call(
        update_kernel,
        grid=(d_out // wide,),
        out_shape=jax.ShapeDtypeStruct((basis.shape[0], d_out), BF16),
        in_specs=[
            pl.BlockSpec(basis.shape, lambda j: (0, 0)),
            pl.BlockSpec((rank, wide), lambda j: (0, j)),
        ],
        out_specs=pl.BlockSpec((basis.shape[0], wide), lambda j: (0, j)),
        compiler_params=pltpu.CompilerParams(vmem_limit_bytes=32 * 1024 * 1024),
        name="back_projection",
    )(basis, direction)
    return grad_in, first_new, second_new, weight_update


def on_device(acts, grad_out, weight, basis, first_moment, second_moment):
    grad_in = lax.dot_general(
        grad_out,
        lax.all_gather(weight, "fsdp", axis=0, tiled=True),
        (((1,), (1,)), ((), ())),
        preferred_element_type=F32,
    ).astype(BF16)
    coords = jnp.dot(
        acts, lax.all_gather(basis, "fsdp", axis=0, tiled=True), preferred_element_type=F32
    ).astype(BF16)
    projected = lax.psum_scatter(
        lax.dot_general(coords, grad_out, (((0,), (0,)), ((), ())), preferred_element_type=F32),
        ("dp", "fsdp"),
        scatter_dimension=0,
        tiled=True,
    )
    total = lax.psum(jnp.sum(projected * projected), ("dp", "fsdp"))
    first_new, second_new, direction = clipped_adam(
        projected, total, first_moment, second_moment, basis.shape[1] * grad_out.shape[1]
    )
    update = jnp.dot(
        basis,
        lax.all_gather(direction, ("dp", "fsdp"), axis=0, tiled=True),
        preferred_element_type=F32,
    )
    return grad_in, first_new, second_new, (0.25 * update).astype(BF16)


def solution(mesh):
    split = P(("dp", "fsdp"), None)
    halves = P("fsdp", None)
    small = mesh.shape["dp"] == 2 * PLANES and mesh.shape["fsdp"] == 2
    return jax.shard_map(
        on_device_kernel if small else on_device,
        mesh=mesh,
        in_specs=(split, split, halves, halves, split, split),
        out_specs=(split, split, split, halves),
        check_vma=False,
    )
```

```python
import functools
import math

import jax
import jax.numpy as jnp
from jax import lax
from jax.experimental import pallas as pl
from jax.experimental.pallas import tpu as pltpu
from jax.sharding import PartitionSpec as P

MESH = pl.DeviceIdType.MESH
F32 = jnp.float32
BF16 = jnp.bfloat16

first_bias = 1.0 - 0.9**10
second_bias = 1.0 - 0.999**10

PLANES = 8
CHUNKS = 4


def clipped_adam(projected, total, first_moment, second_moment, entries):
    limit = math.sqrt(entries)
    factor = jnp.minimum(1.0, limit / (jnp.sqrt(total) + 1e-06))
    clipped = factor * projected
    first_new = 0.9 * first_moment + 0.1 * clipped
    second_new = 0.999 * second_moment + 0.001 * clipped * clipped
    direction = first_new / first_bias / (jnp.sqrt(second_new / second_bias) + 1e-08)
    return first_new, second_new, direction.astype(BF16)


def step_kernel(
    acts_ref, grad_ref, weight_hbm, basis_hbm, first_hbm, second_hbm,
    grad_in_ref, first_out, second_out, gathered_hbm,
    weight, basis_ref, first_ref, second_ref, acts_pair, basis_perm, partial, partial_in, grads, coords,
    own, mine16, arrived, sums_out, sums_in, gathered, back_out, back_in,
    load_sems, out_sem,
    acts_s, acts_r, coords_s, coords_r, gx_s, gx_r, gc_s, gc_r, gf_s, gf_r,
    rs_s, rs_r, sum_s, sum_r, back_s, back_r,
    az_s, az_r, ax_s, ax_r, ac_s, ac_r, af_s, af_r,
):
    dp = lax.axis_index("dp")
    x = lax.axis_index("fsdp")
    ox = 1 - x
    plane = dp // 2
    core = dp % 2
    oc = 1 - core
    me = core * 2 + x
    tokens, d_in = acts_ref.shape
    half = d_in // 2
    d_out = grad_ref.shape[1]
    wide = d_out // CHUNKS
    rank = basis_ref.shape[1]
    quarter = rank // 4
    rows = rank // (4 * PLANES)

    def device(p, c, f):
        return {"dp": p * 2 + c, "fsdp": f}

    partner = device(plane, core, ox)
    sibling = device(plane, oc, x)
    diagonal = device(plane, oc, ox)
    planes = [device((plane + k) % PLANES, core, x) for k in range(PLANES)]
    group = [partner, sibling, diagonal]

    def send(src, dst, s, r, to):
        copy = pltpu.make_async_remote_copy(
            src_ref=src, dst_ref=dst, send_sem=s, recv_sem=r, device_id=to, device_id_type=MESH
        )
        copy.start()
        return copy

    loads = []
    own_half = acts_ref.at[:, pl.ds(pl.multiple_of(x * half, half), half)]
    for src, dst in [
        (basis_hbm, basis_ref), (own_half, acts_pair.at[x]), (grad_ref, grads.at[me]),
        (first_hbm, first_ref), (second_hbm, second_ref), (weight_hbm, weight),
    ]:
        loads.append(pltpu.make_async_copy(src, dst, load_sems.at[len(loads)]))
        loads[-1].start()
    barrier = pltpu.get_barrier_semaphore()
    for to in group + planes[1:]:
        pl.semaphore_signal(barrier, inc=1, device_id=to, device_id_type=MESH)
    pl.semaphore_wait(barrier, 2 + PLANES)

    pending = []
    acts_copy = send(
        acts_ref.at[:, pl.ds(pl.multiple_of(ox * half, half), half)],
        acts_pair.at[x], acts_s, acts_r, partner,
    )
    to_partner = []
    to_sibling = []

    def send_gradient(n):
        cols = pl.ds(n * wide, wide)
        to_partner.append(
            send(grad_ref.at[:, cols], grads.at[me, :, cols], gx_s.at[n], gx_r.at[n], partner)
        )

    send_gradient(0)
    for n in range(CHUNKS):
        cols = pl.ds(n * wide, wide)
        to_sibling.append(
            send(grad_ref.at[:, cols], grads.at[me, :, cols], gc_s.at[n], gc_r.at[n], sibling)
        )

    at = lax.broadcasted_iota(jnp.int32, (rank, rank), 0)
    to = lax.broadcasted_iota(jnp.int32, (rank, rank), 1)
    source = ((to % quarter) // rows * 4 + to // quarter) * rows + to % rows
    shuffle = jnp.where(at == source, 1.0, 0.0).astype(BF16)
    loads[0].wait()
    basis_perm[...] = jnp.dot(basis_ref[...], shuffle, preferred_element_type=F32).astype(BF16)

    def project(block):
        return jnp.dot(block, basis_perm[...], preferred_element_type=F32)

    loads[1].wait()
    values = project(acts_pair[x])
    for q in range(4):
        partial[q, x] = values[:, q * quarter:(q + 1) * quarter]
    acts_copy.wait_recv()
    values = project(acts_pair[ox])
    for q in range(4):
        partial[q, ox] = values[:, q * quarter:(q + 1) * quarter]
    coord_copies = []
    for k, (to_dev, q) in enumerate(
        [(partner, core * 2 + ox), (diagonal, oc * 2 + ox), (sibling, oc * 2 + x)]
    ):
        coord_copies.append(
            send(partial.at[q], partial_in.at[k], coords_s.at[k], coords_r.at[k], to_dev)
        )
    for n in range(1, CHUNKS):
        send_gradient(n)
    loads[2].wait()
    for copy in coord_copies:
        copy.wait_recv()
    coords[core] = (partial[me] + partial_in[0]).astype(BF16)
    coords[oc] = (partial_in[1] + partial_in[2]).astype(BF16)

    scatter = []
    forward = []
    for n in range(CHUNKS):
        cols = pl.ds(n * wide, wide)
        to_partner[n].wait_recv()
        theirs = core * 2 + ox
        forward.append(
            send(grads.at[theirs, :, cols], grads.at[theirs, :, cols], gf_s.at[n], gf_r.at[n], sibling)
        )
        to_sibling[n].wait_recv()
        forward[n].wait_recv()
        chunk = lax.dot_general(
            coords[...].reshape(4 * tokens, quarter),
            grads[:, :, cols].reshape(4 * tokens, wide),
            (((0,), (0,)), ((), ())),
            preferred_element_type=F32,
        )
        chunk = chunk.reshape(PLANES, rows, wide)
        own[:, :, cols] = chunk
        mine16[:, :, cols] = chunk.astype(BF16)
        for k in range(1, PLANES):
            scatter.append(
                send(
                    mine16.at[(plane + k) % PLANES, :, cols], arrived.at[k - 1, :, cols],
                    rs_s.at[n, k - 1], rs_r.at[n, k - 1], planes[k],
                )
            )

    loads[5].wait()

    def input_gradient(block):
        return lax.dot_general(
            block, weight[...], (((1,), (1,)), ((), ())), preferred_element_type=F32
        ).astype(BF16)

    back_out[...] = input_gradient(grads[core * 2 + ox])
    back = send(back_out, back_in, back_s, back_r, partner)
    grad_in_ref[:, pl.ds(pl.multiple_of(x * half, half), half)] = input_gradient(grads[me])

    loads[3].wait()
    loads[4].wait()
    for copy in scatter:
        copy.wait_recv()
    projected = own[plane]
    for k in range(PLANES - 1):
        projected = projected + arrived[k].astype(F32)

    sums_out[0] = jnp.full((8, 128), jnp.sum(projected * projected), F32)
    copies = []
    for k in range(1, PLANES):
        copies.append(
            send(sums_out.at[0], sums_in.at[k - 1], sum_s.at[k - 1], sum_r.at[k - 1], planes[k])
        )
    total = sums_out[0]
    for k in range(PLANES - 1):
        copies[k].wait_recv()
        total = total + sums_in[k]
    sums_out[1] = total
    for k, to_dev in enumerate(group):
        j = PLANES - 1 + k
        copies.append(send(sums_out.at[1], sums_in.at[j], sum_s.at[j], sum_r.at[j], to_dev))
    for k in range(3):
        copies[PLANES - 1 + k].wait_recv()
        total = total + sums_in[PLANES - 1 + k]
    pending += copies

    first_new, second_new, direction = clipped_adam(
        projected, total[0:1, 0:1], first_ref[...], second_ref[...], rank * d_out
    )
    gathered[plane, me] = direction
    across = []
    for k in range(1, PLANES):
        block = gathered.at[plane, me]
        across.append(send(block, block, az_s.at[k - 1], az_r.at[k - 1], planes[k]))
    first_out[...] = first_new
    second_out[...] = second_new
    along = []
    siblings = []
    theirs = core * 2 + ox

    def relay(k):
        at_plane = (plane + PLANES - k) % PLANES
        along[k].wait_recv()
        block = gathered.at[at_plane, theirs]
        siblings.append(send(block, block, af_s.at[k], af_r.at[k], sibling))

    for k in range(PLANES):
        if k:
            across[k - 1].wait_recv()
        at_plane = (plane + PLANES - k) % PLANES
        block = gathered.at[at_plane, me]
        along.append(send(block, block, ax_s.at[k], ax_r.at[k], partner))
        siblings.append(send(block, block, ac_s.at[k], ac_r.at[k], sibling))
        if k:
            relay(k - 1)
    relay(PLANES - 1)
    back.wait_recv()
    grad_in_ref[:, pl.ds(pl.multiple_of(ox * half, half), half)] = back_in[...]
    for copy in siblings:
        copy.wait_recv()
    store = pltpu.make_async_copy(gathered, gathered_hbm, out_sem)
    store.start()
    pending += [acts_copy, back] + to_partner + to_sibling + coord_copies + forward
    pending += scatter + across + along + siblings
    for copy in pending:
        copy.wait_send()
    store.wait()


def update_kernel(basis_ref, direction_ref, *refs):
    *results, out_ref = refs
    kept = len(results) // 2
    for src, dst in zip(results[:kept], results[kept:]):
        dst[...] = src[...]
    update = jnp.dot(basis_ref[...], direction_ref[...], preferred_element_type=F32)
    out_ref[...] = (0.25 * update).astype(BF16)


def on_device_kernel(acts, grad_out, weight, basis, first_moment, second_moment):
    tokens, d_in = acts.shape
    d_out = grad_out.shape[1]
    half = d_in // 2
    rank = basis.shape[1]
    quarter = rank // 4
    rows = rank // (4 * PLANES)
    vmem = pl.BlockSpec(memory_space=pltpu.VMEM)
    anywhere = pl.BlockSpec(memory_space=pltpu.HBM)
    dma = pltpu.SemaphoreType.DMA
    grad_in, first_new, second_new, direction = pl.pallas_call(
        step_kernel,
        out_shape=(
            jax.ShapeDtypeStruct((tokens, d_in), BF16),
            jax.ShapeDtypeStruct(first_moment.shape, F32),
            jax.ShapeDtypeStruct(second_moment.shape, F32),
            jax.ShapeDtypeStruct((PLANES, 4, rows, d_out), BF16),
        ),
        in_specs=[anywhere] * 6,
        out_specs=(vmem, vmem, vmem, pl.BlockSpec(memory_space=pl.ANY)),
        scratch_shapes=[
            pltpu.VMEM(weight.shape, BF16),
            pltpu.VMEM(basis.shape, BF16),
            pltpu.VMEM(first_moment.shape, F32),
            pltpu.VMEM(second_moment.shape, F32),
            pltpu.VMEM((2, tokens, half), BF16),
            pltpu.VMEM(basis.shape, BF16),
            pltpu.VMEM((4, 2, tokens, quarter), F32),
            pltpu.VMEM((3, 2, tokens, quarter), F32),
            pltpu.VMEM((4, tokens, d_out), BF16),
            pltpu.VMEM((2, 2, tokens, quarter), BF16),
            pltpu.VMEM((PLANES, rows, d_out), F32),
            pltpu.VMEM((PLANES, rows, d_out), BF16),
            pltpu.VMEM((PLANES - 1, rows, d_out), BF16),
            pltpu.VMEM((2, 8, 128), F32),
            pltpu.VMEM((PLANES + 2, 8, 128), F32),
            pltpu.VMEM((PLANES, 4, rows, d_out), BF16),
            pltpu.VMEM((tokens, half), BF16),
            pltpu.VMEM((tokens, half), BF16),
            dma((6,)), dma,
            dma, dma, dma((3,)), dma((3,)),
            dma((CHUNKS,)), dma((CHUNKS,)), dma((CHUNKS,)), dma((CHUNKS,)),
            dma((CHUNKS,)), dma((CHUNKS,)),
            dma((CHUNKS, PLANES - 1)), dma((CHUNKS, PLANES - 1)),
            dma((PLANES + 2,)), dma((PLANES + 2,)), dma, dma,
            dma((PLANES - 1,)), dma((PLANES - 1,)),
            dma((PLANES,)), dma((PLANES,)), dma((PLANES,)), dma((PLANES,)),
            dma((PLANES,)), dma((PLANES,)),
        ],
        compiler_params=pltpu.CompilerParams(
            collective_id=0, has_side_effects=True, vmem_limit_bytes=64 * 1024 * 1024
        ),
        name="galore_step",
    )(acts, grad_out, weight, basis, first_moment, second_moment)
    direction = direction.reshape(rank, d_out)
    wide = 512
    results = (grad_in, first_new, second_new)
    blocks = [pl.BlockSpec((r.shape[0], wide), lambda j: (0, j)) for r in results]
    *results, weight_update = pl.pallas_call(
        update_kernel,
        grid=(d_out // wide,),
        out_shape=[jax.ShapeDtypeStruct(r.shape, r.dtype) for r in results]
        + [jax.ShapeDtypeStruct((basis.shape[0], d_out), BF16)],
        in_specs=[
            pl.BlockSpec(basis.shape, lambda j: (0, 0)),
            pl.BlockSpec((rank, wide), lambda j: (0, j)),
        ]
        + blocks,
        out_specs=blocks + [pl.BlockSpec((basis.shape[0], wide), lambda j: (0, j))],
        compiler_params=pltpu.CompilerParams(vmem_limit_bytes=64 * 1024 * 1024),
        name="back_projection",
    )(basis, direction, *results)
    return *results, weight_update


def on_device(acts, grad_out, weight, basis, first_moment, second_moment):
    grad_in = lax.dot_general(
        grad_out,
        lax.all_gather(weight, "fsdp", axis=0, tiled=True),
        (((1,), (1,)), ((), ())),
        preferred_element_type=F32,
    ).astype(BF16)
    coords = jnp.dot(
        acts, lax.all_gather(basis, "fsdp", axis=0, tiled=True), preferred_element_type=F32
    ).astype(BF16)
    projected = lax.psum_scatter(
        lax.dot_general(coords, grad_out, (((0,), (0,)), ((), ())), preferred_element_type=F32),
        ("dp", "fsdp"),
        scatter_dimension=0,
        tiled=True,
    )
    total = lax.psum(jnp.sum(projected * projected), ("dp", "fsdp"))
    first_new, second_new, direction = clipped_adam(
        projected, total, first_moment, second_moment, basis.shape[1] * grad_out.shape[1]
    )
    update = jnp.dot(
        basis,
        lax.all_gather(direction, ("dp", "fsdp"), axis=0, tiled=True),
        preferred_element_type=F32,
    )
    return grad_in, first_new, second_new, (0.25 * update).astype(BF16)


def solution(mesh):
    split = P(("dp", "fsdp"), None)
    halves = P("fsdp", None)
    small = mesh.shape["dp"] == 2 * PLANES and mesh.shape["fsdp"] == 2
    return jax.shard_map(
        on_device_kernel if small else on_device,
        mesh=mesh,
        in_specs=(split, split, halves, halves, split, split),
        out_specs=(split, split, split, halves),
        check_vma=False,
    )
```

```python
import functools
import math

import jax
import jax.numpy as jnp
from jax import lax
from jax.experimental import pallas as pl
from jax.experimental.pallas import tpu as pltpu
from jax.sharding import PartitionSpec as P

MESH = pl.DeviceIdType.MESH
F32 = jnp.float32
BF16 = jnp.bfloat16

first_bias = 1.0 - 0.9**10
second_bias = 1.0 - 0.999**10

PLANES = 8
DEPTH = PLANES // 2
CHUNKS = 4


def clipped_adam(projected, total, first_moment, second_moment, entries):
    limit = math.sqrt(entries)
    factor = jnp.minimum(1.0, limit / (jnp.sqrt(total) + 1e-06))
    clipped = factor * projected
    first_new = 0.9 * first_moment + 0.1 * clipped
    second_new = 0.999 * second_moment + 0.001 * clipped * clipped
    direction = first_new / first_bias / (jnp.sqrt(second_new / second_bias) + 1e-08)
    return first_new, second_new, direction.astype(BF16)


def step_kernel(
    acts_ref, grad_ref, weight_hbm, basis_hbm, first_hbm, second_hbm,
    grad_in_ref, first_out, second_out, gathered_hbm,
    weight, basis_ref, first_ref, second_ref, acts_pair, basis_perm, partial, partial_in, grads, coords,
    feature, own, mine16, arrived, sums_out, sums_in, gathered, back_out, back_in,
    load_sems, out_sem,
    acts_s, acts_r, coords_s, coords_r, gx_s, gx_r, gc_s, gc_r, gf_s, gf_r,
    rs_s, rs_r, sum_s, sum_r, back_s, back_r,
    gather_s, gather_r,
):
    dp = lax.axis_index("dp")
    x = lax.axis_index("fsdp")
    ox = 1 - x
    plane = dp // 2
    core = dp % 2
    oc = 1 - core
    me = core * 2 + x
    tokens, d_in = acts_ref.shape
    half = d_in // 2
    d_out = grad_ref.shape[1]
    wide = d_out // CHUNKS
    rank = basis_ref.shape[1]
    quarter = rank // 4
    rows = rank // (4 * PLANES)

    def device(p, c, f):
        return {"dp": p * 2 + c, "fsdp": f}

    partner = device(plane, core, ox)
    sibling = device(plane, oc, x)
    diagonal = device(plane, oc, ox)
    planes = [device((plane + k) % PLANES, core, x) for k in range(PLANES)]
    group = [partner, sibling, diagonal]

    def send(src, dst, s, r, to):
        copy = pltpu.make_async_remote_copy(
            src_ref=src, dst_ref=dst, send_sem=s, recv_sem=r, device_id=to, device_id_type=MESH
        )
        copy.start()
        return copy

    loads = []
    own_half = acts_ref.at[:, pl.ds(pl.multiple_of(x * half, half), half)]
    for src, dst in [
        (basis_hbm, basis_ref), (own_half, acts_pair.at[x]), (grad_ref, grads.at[me]),
        (first_hbm, first_ref), (second_hbm, second_ref), (weight_hbm, weight),
    ]:
        loads.append(pltpu.make_async_copy(src, dst, load_sems.at[len(loads)]))
        loads[-1].start()
    barrier = pltpu.get_barrier_semaphore()
    for to in group + planes[1:]:
        pl.semaphore_signal(barrier, inc=1, device_id=to, device_id_type=MESH)
    pl.semaphore_wait(barrier, 2 + PLANES)

    pending = []
    acts_copy = send(
        acts_ref.at[:, pl.ds(pl.multiple_of(ox * half, half), half)],
        acts_pair.at[x], acts_s, acts_r, partner,
    )
    to_partner = []
    to_sibling = []

    def send_gradient(n):
        cols = pl.ds(n * wide, wide)
        to_partner.append(
            send(grad_ref.at[:, cols], grads.at[me, :, cols], gx_s.at[n], gx_r.at[n], partner)
        )

    send_gradient(0)
    for n in range(CHUNKS):
        cols = pl.ds(n * wide, wide)
        to_sibling.append(
            send(grad_ref.at[:, cols], grads.at[me, :, cols], gc_s.at[n], gc_r.at[n], sibling)
        )

    at = lax.broadcasted_iota(jnp.int32, (rank, rank), 0)
    to = lax.broadcasted_iota(jnp.int32, (rank, rank), 1)
    source = ((to % quarter) // rows * 4 + to // quarter) * rows + to % rows
    shuffle = jnp.where(at == source, 1.0, 0.0).astype(BF16)
    loads[0].wait()
    basis_perm[...] = jnp.dot(basis_ref[...], shuffle, preferred_element_type=F32).astype(BF16)

    def project(block):
        return jnp.dot(block, basis_perm[...], preferred_element_type=F32)

    loads[1].wait()
    values = project(acts_pair[x])
    for q in range(4):
        partial[q, x] = values[:, q * quarter:(q + 1) * quarter]
    acts_copy.wait_recv()
    values = project(acts_pair[ox])
    for q in range(4):
        partial[q, ox] = values[:, q * quarter:(q + 1) * quarter]
    coord_copies = []
    for k, (to_dev, q) in enumerate(
        [(partner, core * 2 + ox), (diagonal, oc * 2 + ox), (sibling, oc * 2 + x)]
    ):
        coord_copies.append(
            send(partial.at[q], partial_in.at[k], coords_s.at[k], coords_r.at[k], to_dev)
        )
    for n in range(1, CHUNKS):
        send_gradient(n)
    loads[2].wait()
    for copy in coord_copies:
        copy.wait_recv()
    coords[core] = (partial[me] + partial_in[0]).astype(BF16)
    coords[oc] = (partial_in[1] + partial_in[2]).astype(BF16)

    loads[5].wait()
    scatter = []
    forward = []
    for n in range(CHUNKS):
        cols = pl.ds(n * wide, wide)
        to_partner[n].wait_recv()
        theirs = core * 2 + ox
        forward.append(
            send(grads.at[theirs, :, cols], grads.at[theirs, :, cols], gf_s.at[n], gf_r.at[n], sibling)
        )
        to_sibling[n].wait_recv()
        forward[n].wait_recv()
        chunk = lax.dot_general(
            coords[...].reshape(4 * tokens, quarter),
            grads[:, :, cols].reshape(4 * tokens, wide),
            (((0,), (0,)), ((), ())),
            preferred_element_type=F32,
        )
        chunk = chunk.reshape(PLANES, rows, wide)
        own[:, :, cols] = chunk
        mine16[:, :, cols] = chunk.astype(BF16)
        for k in range(1, PLANES):
            scatter.append(
                send(
                    mine16.at[(plane + k) % PLANES, :, cols], arrived.at[k - 1, :, cols],
                    rs_s.at[n, k - 1], rs_r.at[n, k - 1], planes[k],
                )
            )
        term = lax.dot_general(
            grads[pl.ds(core * 2, 2), :, cols].reshape(2 * tokens, wide),
            weight[:, cols],
            (((1,), (1,)), ((), ())),
            preferred_element_type=F32,
        ).reshape(2, tokens, half)
        if n == 0:
            feature[...] = term
        else:
            feature[...] += term

    back_out[...] = feature[ox].astype(BF16)
    back = send(back_out, back_in, back_s, back_r, partner)
    grad_in_ref[:, pl.ds(pl.multiple_of(x * half, half), half)] = feature[x].astype(BF16)

    loads[3].wait()
    loads[4].wait()
    for copy in scatter:
        copy.wait_recv()
    projected = own[plane]
    for k in range(PLANES - 1):
        projected = projected + arrived[k].astype(F32)

    sums_out[0] = jnp.full((8, 128), jnp.sum(projected * projected), F32)
    sums = []
    for k in range(1, PLANES):
        sums.append(
            send(sums_out.at[0], sums_in.at[k - 1], sum_s.at[k - 1], sum_r.at[k - 1], planes[k])
        )
    total = sums_out[0]
    for k in range(PLANES - 1):
        sums[k].wait_recv()
        total = total + sums_in[k]
    sums_out[1] = total
    for k, to_dev in enumerate(group):
        j = PLANES - 1 + k
        sums.append(send(sums_out.at[1], sums_in.at[j], sum_s.at[j], sum_r.at[j], to_dev))
    for k in range(3):
        sums[PLANES - 1 + k].wait_recv()
        total = total + sums_in[PLANES - 1 + k]
    pending += sums

    first_new, second_new, direction = clipped_adam(
        projected, total[0:1, 0:1], first_ref[...], second_ref[...], rank * d_out
    )
    gathered[plane, me] = direction
    z = plane // 2
    y = plane % 2
    oy = 1 - y
    theirs = core * 2 + ox
    beside = device(z * 2 + oy, core, x)
    left = pl.ds(0, d_out // 2)
    right = pl.ds(d_out // 2, d_out // 2)
    copies = {}

    def pass_on(kind, j, block, to_dev):
        copies[kind, j] = send(block, block, gather_s.at[kind, j], gather_r.at[kind, j], to_dev)

    for j in range(1, DEPTH):
        pass_on(0, j, gathered.at[plane, me], device((z + j) % DEPTH * 2 + y, core, x))

    def spread(j):
        if j:
            copies[0, j].wait_recv()
        block = gathered.at[(z + DEPTH - j) % DEPTH * 2 + y, me]
        pass_on(1, j, block, beside)
        pass_on(2, j, block, partner)
        pass_on(3, j, block, sibling)

    def relay(j):
        at_z = (z + DEPTH - j) % DEPTH * 2
        copies[1, j].wait_recv()
        pass_on(4, j, gathered.at[at_z + oy, me, :, left], partner)
        pass_on(5, j, gathered.at[at_z + oy, me], sibling)
        copies[2, j].wait_recv()
        pass_on(6, j, gathered.at[at_z + y, theirs, :, right], beside)
        pass_on(7, j, gathered.at[at_z + y, theirs], sibling)

    def corner(j):
        copies[4, j].wait_recv()
        copies[6, j].wait_recv()
        pass_on(8, j, gathered.at[(z + DEPTH - j) % DEPTH * 2 + oy, theirs], sibling)

    spread(0)
    first_out[...] = first_new
    second_out[...] = second_new
    for j in range(1, DEPTH + 2):
        if j < DEPTH:
            spread(j)
        if j <= DEPTH:
            relay(j - 1)
        if j >= 2:
            corner(j - 2)
    back.wait_recv()
    grad_in_ref[:, pl.ds(pl.multiple_of(ox * half, half), half)] = back_in[...]
    for kind in (3, 5, 7, 8):
        for j in range(DEPTH):
            copies[kind, j].wait_recv()
    store = pltpu.make_async_copy(gathered, gathered_hbm, out_sem)
    store.start()
    pending += [acts_copy, back] + to_partner + to_sibling + coord_copies + forward
    pending += scatter + list(copies.values())
    for copy in pending:
        copy.wait_send()
    store.wait()


def update_kernel(basis_ref, direction_ref, *refs):
    *results, out_ref = refs
    kept = len(results) // 2
    for src, dst in zip(results[:kept], results[kept:]):
        dst[...] = src[...]
    update = jnp.dot(basis_ref[...], direction_ref[...], preferred_element_type=F32)
    out_ref[...] = (0.25 * update).astype(BF16)


def on_device_kernel(acts, grad_out, weight, basis, first_moment, second_moment):
    tokens, d_in = acts.shape
    d_out = grad_out.shape[1]
    half = d_in // 2
    rank = basis.shape[1]
    quarter = rank // 4
    rows = rank // (4 * PLANES)
    vmem = pl.BlockSpec(memory_space=pltpu.VMEM)
    anywhere = pl.BlockSpec(memory_space=pltpu.HBM)
    dma = pltpu.SemaphoreType.DMA
    grad_in, first_new, second_new, direction = pl.pallas_call(
        step_kernel,
        out_shape=(
            jax.ShapeDtypeStruct((tokens, d_in), BF16),
            jax.ShapeDtypeStruct(first_moment.shape, F32),
            jax.ShapeDtypeStruct(second_moment.shape, F32),
            jax.ShapeDtypeStruct((PLANES, 4, rows, d_out), BF16),
        ),
        in_specs=[anywhere] * 6,
        out_specs=(vmem, vmem, vmem, pl.BlockSpec(memory_space=pl.ANY)),
        scratch_shapes=[
            pltpu.VMEM(weight.shape, BF16),
            pltpu.VMEM(basis.shape, BF16),
            pltpu.VMEM(first_moment.shape, F32),
            pltpu.VMEM(second_moment.shape, F32),
            pltpu.VMEM((2, tokens, half), BF16),
            pltpu.VMEM(basis.shape, BF16),
            pltpu.VMEM((4, 2, tokens, quarter), F32),
            pltpu.VMEM((3, 2, tokens, quarter), F32),
            pltpu.VMEM((4, tokens, d_out), BF16),
            pltpu.VMEM((2, 2, tokens, quarter), BF16),
            pltpu.VMEM((2, tokens, half), F32),
            pltpu.VMEM((PLANES, rows, d_out), F32),
            pltpu.VMEM((PLANES, rows, d_out), BF16),
            pltpu.VMEM((PLANES - 1, rows, d_out), BF16),
            pltpu.VMEM((2, 8, 128), F32),
            pltpu.VMEM((PLANES + 2, 8, 128), F32),
            pltpu.VMEM((PLANES, 4, rows, d_out), BF16),
            pltpu.VMEM((tokens, half), BF16),
            pltpu.VMEM((tokens, half), BF16),
            dma((6,)), dma,
            dma, dma, dma((3,)), dma((3,)),
            dma((CHUNKS,)), dma((CHUNKS,)), dma((CHUNKS,)), dma((CHUNKS,)),
            dma((CHUNKS,)), dma((CHUNKS,)),
            dma((CHUNKS, PLANES - 1)), dma((CHUNKS, PLANES - 1)),
            dma((PLANES + 2,)), dma((PLANES + 2,)), dma, dma,
            dma((9, DEPTH)), dma((9, DEPTH)),
        ],
        compiler_params=pltpu.CompilerParams(
            collective_id=0, has_side_effects=True, vmem_limit_bytes=64 * 1024 * 1024
        ),
        name="galore_step",
    )(acts, grad_out, weight, basis, first_moment, second_moment)
    direction = direction.reshape(rank, d_out)
    wide = 512
    results = (grad_in, first_new, second_new)
    blocks = [pl.BlockSpec((r.shape[0], wide), lambda j: (0, j)) for r in results]
    *results, weight_update = pl.pallas_call(
        update_kernel,
        grid=(d_out // wide,),
        out_shape=[jax.ShapeDtypeStruct(r.shape, r.dtype) for r in results]
        + [jax.ShapeDtypeStruct((basis.shape[0], d_out), BF16)],
        in_specs=[
            pl.BlockSpec(basis.shape, lambda j: (0, 0)),
            pl.BlockSpec((rank, wide), lambda j: (0, j)),
        ]
        + blocks,
        out_specs=blocks + [pl.BlockSpec((basis.shape[0], wide), lambda j: (0, j))],
        compiler_params=pltpu.CompilerParams(vmem_limit_bytes=64 * 1024 * 1024),
        name="back_projection",
    )(basis, direction, *results)
    return *results, weight_update


def on_device(acts, grad_out, weight, basis, first_moment, second_moment):
    grad_in = lax.dot_general(
        grad_out,
        lax.all_gather(weight, "fsdp", axis=0, tiled=True),
        (((1,), (1,)), ((), ())),
        preferred_element_type=F32,
    ).astype(BF16)
    coords = jnp.dot(
        acts, lax.all_gather(basis, "fsdp", axis=0, tiled=True), preferred_element_type=F32
    ).astype(BF16)
    projected = lax.psum_scatter(
        lax.dot_general(coords, grad_out, (((0,), (0,)), ((), ())), preferred_element_type=F32),
        ("dp", "fsdp"),
        scatter_dimension=0,
        tiled=True,
    )
    total = lax.psum(jnp.sum(projected * projected), ("dp", "fsdp"))
    first_new, second_new, direction = clipped_adam(
        projected, total, first_moment, second_moment, basis.shape[1] * grad_out.shape[1]
    )
    update = jnp.dot(
        basis,
        lax.all_gather(direction, ("dp", "fsdp"), axis=0, tiled=True),
        preferred_element_type=F32,
    )
    return grad_in, first_new, second_new, (0.25 * update).astype(BF16)


def solution(mesh):
    split = P(("dp", "fsdp"), None)
    halves = P("fsdp", None)
    small = mesh.shape["dp"] == 2 * PLANES and mesh.shape["fsdp"] == 2
    return jax.shard_map(
        on_device_kernel if small else on_device,
        mesh=mesh,
        in_specs=(split, split, halves, halves, split, split),
        out_specs=(split, split, split, halves),
        check_vma=False,
    )
```

```python
import functools
import math

import jax
import jax.numpy as jnp
from jax import lax
from jax.experimental import pallas as pl
from jax.experimental.pallas import tpu as pltpu
from jax.sharding import PartitionSpec as P

MESH = pl.DeviceIdType.MESH
F32 = jnp.float32
BF16 = jnp.bfloat16

first_bias = 1.0 - 0.9**10
second_bias = 1.0 - 0.999**10

PLANES = 8
DEPTH = PLANES // 2
CHUNKS = 4


def clipped_adam(projected, total, first_moment, second_moment, entries):
    limit = math.sqrt(entries)
    factor = jnp.minimum(1.0, limit / (jnp.sqrt(total) + 1e-06))
    clipped = factor * projected
    first_new = 0.9 * first_moment + 0.1 * clipped
    second_new = 0.999 * second_moment + 0.001 * clipped * clipped
    direction = first_new / first_bias / (jnp.sqrt(second_new / second_bias) + 1e-08)
    return first_new, second_new, direction.astype(BF16)


def step_kernel(
    acts_ref, grad_ref, weight_hbm, basis_hbm, first_hbm, second_hbm,
    grad_in_ref, first_out, second_out, gathered_hbm,
    weight, basis_ref, first_ref, second_ref, acts_pair, basis_perm, partial, partial_in, grads, coords,
    feature, own, mine16, from_y, pairs, pairs16, arrived, sums_out, sums_in, gathered, back_out, back_in,
    load_sems, out_sem,
    acts_s, acts_r, coords_s, coords_r, gx_s, gx_r, gc_s, gc_r, gf_s, gf_r,
    ry_s, ry_r, rs_s, rs_r, sum_s, sum_r, back_s, back_r,
    gather_s, gather_r,
):
    dp = lax.axis_index("dp")
    x = lax.axis_index("fsdp")
    ox = 1 - x
    plane = dp // 2
    core = dp % 2
    oc = 1 - core
    me = core * 2 + x
    tokens, d_in = acts_ref.shape
    half = d_in // 2
    d_out = grad_ref.shape[1]
    wide = d_out // CHUNKS
    rank = basis_ref.shape[1]
    quarter = rank // 4
    rows = rank // (4 * PLANES)

    def device(p, c, f):
        return {"dp": p * 2 + c, "fsdp": f}

    partner = device(plane, core, ox)
    sibling = device(plane, oc, x)
    diagonal = device(plane, oc, ox)
    planes = [device((plane + k) % PLANES, core, x) for k in range(PLANES)]
    group = [partner, sibling, diagonal]

    def send(src, dst, s, r, to):
        copy = pltpu.make_async_remote_copy(
            src_ref=src, dst_ref=dst, send_sem=s, recv_sem=r, device_id=to, device_id_type=MESH
        )
        copy.start()
        return copy

    loads = []
    own_half = acts_ref.at[:, pl.ds(pl.multiple_of(x * half, half), half)]
    for src, dst in [
        (basis_hbm, basis_ref), (own_half, acts_pair.at[x]), (grad_ref, grads.at[me]),
        (first_hbm, first_ref), (second_hbm, second_ref), (weight_hbm, weight),
    ]:
        loads.append(pltpu.make_async_copy(src, dst, load_sems.at[len(loads)]))
        loads[-1].start()
    barrier = pltpu.get_barrier_semaphore()
    for to in group + planes[1:]:
        pl.semaphore_signal(barrier, inc=1, device_id=to, device_id_type=MESH)
    pl.semaphore_wait(barrier, 2 + PLANES)

    pending = []
    acts_copy = send(
        acts_ref.at[:, pl.ds(pl.multiple_of(ox * half, half), half)],
        acts_pair.at[x], acts_s, acts_r, partner,
    )
    to_partner = []
    to_sibling = []

    def send_gradient(n):
        cols = pl.ds(n * wide, wide)
        to_partner.append(
            send(grad_ref.at[:, cols], grads.at[me, :, cols], gx_s.at[n], gx_r.at[n], partner)
        )

    for n in range(CHUNKS):
        cols = pl.ds(n * wide, wide)
        to_sibling.append(
            send(grad_ref.at[:, cols], grads.at[me, :, cols], gc_s.at[n], gc_r.at[n], sibling)
        )

    at = lax.broadcasted_iota(jnp.int32, (rank, rank), 0)
    to = lax.broadcasted_iota(jnp.int32, (rank, rank), 1)
    source = ((to % quarter) // rows * 4 + to // quarter) * rows + to % rows
    shuffle = jnp.where(at == source, 1.0, 0.0).astype(BF16)
    loads[0].wait()
    basis_perm[...] = jnp.dot(basis_ref[...], shuffle, preferred_element_type=F32).astype(BF16)

    def project(block):
        return jnp.dot(block, basis_perm[...], preferred_element_type=F32)

    loads[1].wait()
    values = project(acts_pair[x])
    for q in range(4):
        partial[q, x] = values[:, q * quarter:(q + 1) * quarter]
    acts_copy.wait_send()
    send_gradient(0)
    acts_copy.wait_recv()
    values = project(acts_pair[ox])
    for q in range(4):
        partial[q, ox] = values[:, q * quarter:(q + 1) * quarter]
    coord_copies = []
    for k, (to_dev, q) in enumerate(
        [(partner, core * 2 + ox), (diagonal, oc * 2 + ox), (sibling, oc * 2 + x)]
    ):
        coord_copies.append(
            send(partial.at[q], partial_in.at[k], coords_s.at[k], coords_r.at[k], to_dev)
        )
    send_gradient(1)
    loads[2].wait()
    for copy in coord_copies:
        copy.wait_recv()
    send_gradient(2)
    coords[core] = (partial[me] + partial_in[0]).astype(BF16)
    coords[oc] = (partial_in[1] + partial_in[2]).astype(BF16)

    loads[5].wait()
    z = plane // 2
    y = plane % 2
    oy = 1 - y
    beside = device(z * 2 + oy, core, x)
    over_y = []
    scatter = []
    forward = []

    def reduce_z(n):
        cols = pl.ds(n * wide, wide)
        over_y[n].wait_recv()
        pair = own[:, y, :, cols] + from_y[:, :, cols].astype(F32)
        pairs[:, :, cols] = pair
        pairs16[:, :, cols] = pair.astype(BF16)
        for k in range(1, DEPTH):
            scatter.append(
                send(
                    pairs16.at[(z + k) % DEPTH, :, cols], arrived.at[k - 1, :, cols],
                    rs_s.at[n, k - 1], rs_r.at[n, k - 1], device((z + k) % DEPTH * 2 + y, core, x),
                )
            )

    for n in range(CHUNKS):
        cols = pl.ds(n * wide, wide)
        to_partner[n].wait_recv()
        if n + 3 < CHUNKS:
            send_gradient(n + 3)
        theirs = core * 2 + ox
        forward.append(
            send(grads.at[theirs, :, cols], grads.at[theirs, :, cols], gf_s.at[n], gf_r.at[n], sibling)
        )
        to_sibling[n].wait_recv()
        forward[n].wait_recv()
        chunk = lax.dot_general(
            coords[...].reshape(4 * tokens, quarter),
            grads[:, :, cols].reshape(4 * tokens, wide),
            (((0,), (0,)), ((), ())),
            preferred_element_type=F32,
        )
        chunk = chunk.reshape(DEPTH, 2, rows, wide)
        own[:, :, :, cols] = chunk
        mine16[:, :, :, cols] = chunk.astype(BF16)
        over_y.append(
            send(
                mine16.at[:, oy, :, cols], from_y.at[:, :, cols], ry_s.at[n], ry_r.at[n], beside
            )
        )
        if n:
            reduce_z(n - 1)
        term = lax.dot_general(
            grads[pl.ds(core * 2, 2), :, cols].reshape(2 * tokens, wide),
            weight[:, cols],
            (((1,), (1,)), ((), ())),
            preferred_element_type=F32,
        ).reshape(2, tokens, half)
        if n == 0:
            feature[...] = term
        else:
            feature[...] += term

    reduce_z(CHUNKS - 1)
    back_out[...] = feature[ox].astype(BF16)
    back = send(back_out, back_in, back_s, back_r, partner)
    grad_in_ref[:, pl.ds(pl.multiple_of(x * half, half), half)] = feature[x].astype(BF16)

    loads[3].wait()
    loads[4].wait()
    for copy in scatter:
        copy.wait_recv()
    projected = pairs[z]
    for k in range(DEPTH - 1):
        projected = projected + arrived[k].astype(F32)

    sums_out[0] = jnp.full((8, 128), jnp.sum(projected * projected), F32)
    sums = []
    for k in range(1, PLANES):
        sums.append(
            send(sums_out.at[0], sums_in.at[k - 1], sum_s.at[k - 1], sum_r.at[k - 1], planes[k])
        )
    total = sums_out[0]
    for k in range(PLANES - 1):
        sums[k].wait_recv()
        total = total + sums_in[k]
    sums_out[1] = total
    for k, to_dev in enumerate(group):
        j = PLANES - 1 + k
        sums.append(send(sums_out.at[1], sums_in.at[j], sum_s.at[j], sum_r.at[j], to_dev))
    for k in range(3):
        sums[PLANES - 1 + k].wait_recv()
        total = total + sums_in[PLANES - 1 + k]
    pending += sums

    first_new, second_new, direction = clipped_adam(
        projected, total[0:1, 0:1], first_ref[...], second_ref[...], rank * d_out
    )
    gathered[plane, me] = direction
    theirs = core * 2 + ox
    left = pl.ds(0, d_out // 2)
    right = pl.ds(d_out // 2, d_out // 2)
    copies = {}

    def pass_on(kind, j, block, to_dev):
        copies[kind, j] = send(block, block, gather_s.at[kind, j], gather_r.at[kind, j], to_dev)

    for j in range(1, DEPTH):
        pass_on(0, j, gathered.at[plane, me], device((z + j) % DEPTH * 2 + y, core, x))

    def spread(j):
        if j:
            copies[0, j].wait_recv()
        block = gathered.at[(z + DEPTH - j) % DEPTH * 2 + y, me]
        pass_on(1, j, block, beside)
        pass_on(2, j, block, partner)
        pass_on(3, j, block, sibling)

    def relay(j):
        at_z = (z + DEPTH - j) % DEPTH * 2
        copies[1, j].wait_recv()
        pass_on(4, j, gathered.at[at_z + oy, me, :, left], partner)
        pass_on(5, j, gathered.at[at_z + oy, me], sibling)
        copies[2, j].wait_recv()
        pass_on(6, j, gathered.at[at_z + y, theirs, :, right], beside)
        pass_on(7, j, gathered.at[at_z + y, theirs], sibling)

    def corner(j):
        copies[4, j].wait_recv()
        copies[6, j].wait_recv()
        pass_on(8, j, gathered.at[(z + DEPTH - j) % DEPTH * 2 + oy, theirs], sibling)

    spread(0)
    first_out[...] = first_new
    second_out[...] = second_new
    for j in range(1, DEPTH + 2):
        if j < DEPTH:
            spread(j)
        if j <= DEPTH:
            relay(j - 1)
        if j >= 2:
            corner(j - 2)
    back.wait_recv()
    grad_in_ref[:, pl.ds(pl.multiple_of(ox * half, half), half)] = back_in[...]
    for kind in (3, 5, 7, 8):
        for j in range(DEPTH):
            copies[kind, j].wait_recv()
    store = pltpu.make_async_copy(gathered, gathered_hbm, out_sem)
    store.start()
    pending += [back] + to_partner + to_sibling + coord_copies + forward
    pending += over_y + scatter + list(copies.values())
    for copy in pending:
        copy.wait_send()
    store.wait()


def update_kernel(basis_ref, direction_ref, *refs):
    *results, out_ref = refs
    kept = len(results) // 2
    for src, dst in zip(results[:kept], results[kept:]):
        dst[...] = src[...]
    update = jnp.dot(basis_ref[...], direction_ref[...], preferred_element_type=F32)
    out_ref[...] = (0.25 * update).astype(BF16)


def on_device_kernel(acts, grad_out, weight, basis, first_moment, second_moment):
    tokens, d_in = acts.shape
    d_out = grad_out.shape[1]
    half = d_in // 2
    rank = basis.shape[1]
    quarter = rank // 4
    rows = rank // (4 * PLANES)
    vmem = pl.BlockSpec(memory_space=pltpu.VMEM)
    anywhere = pl.BlockSpec(memory_space=pltpu.HBM)
    dma = pltpu.SemaphoreType.DMA
    grad_in, first_new, second_new, direction = pl.pallas_call(
        step_kernel,
        out_shape=(
            jax.ShapeDtypeStruct((tokens, d_in), BF16),
            jax.ShapeDtypeStruct(first_moment.shape, F32),
            jax.ShapeDtypeStruct(second_moment.shape, F32),
            jax.ShapeDtypeStruct((PLANES, 4, rows, d_out), BF16),
        ),
        in_specs=[anywhere] * 6,
        out_specs=(vmem, vmem, vmem, pl.BlockSpec(memory_space=pl.ANY)),
        scratch_shapes=[
            pltpu.VMEM(weight.shape, BF16),
            pltpu.VMEM(basis.shape, BF16),
            pltpu.VMEM(first_moment.shape, F32),
            pltpu.VMEM(second_moment.shape, F32),
            pltpu.VMEM((2, tokens, half), BF16),
            pltpu.VMEM(basis.shape, BF16),
            pltpu.VMEM((4, 2, tokens, quarter), F32),
            pltpu.VMEM((3, 2, tokens, quarter), F32),
            pltpu.VMEM((4, tokens, d_out), BF16),
            pltpu.VMEM((2, 2, tokens, quarter), BF16),
            pltpu.VMEM((2, tokens, half), F32),
            pltpu.VMEM((DEPTH, 2, rows, d_out), F32),
            pltpu.VMEM((DEPTH, 2, rows, d_out), BF16),
            pltpu.VMEM((DEPTH, rows, d_out), BF16),
            pltpu.VMEM((DEPTH, rows, d_out), F32),
            pltpu.VMEM((DEPTH, rows, d_out), BF16),
            pltpu.VMEM((DEPTH - 1, rows, d_out), BF16),
            pltpu.VMEM((2, 8, 128), F32),
            pltpu.VMEM((PLANES + 2, 8, 128), F32),
            pltpu.VMEM((PLANES, 4, rows, d_out), BF16),
            pltpu.VMEM((tokens, half), BF16),
            pltpu.VMEM((tokens, half), BF16),
            dma((6,)), dma,
            dma, dma, dma((3,)), dma((3,)),
            dma((CHUNKS,)), dma((CHUNKS,)), dma((CHUNKS,)), dma((CHUNKS,)),
            dma((CHUNKS,)), dma((CHUNKS,)),
            dma((CHUNKS,)), dma((CHUNKS,)),
            dma((CHUNKS, DEPTH - 1)), dma((CHUNKS, DEPTH - 1)),
            dma((PLANES + 2,)), dma((PLANES + 2,)), dma, dma,
            dma((9, DEPTH)), dma((9, DEPTH)),
        ],
        compiler_params=pltpu.CompilerParams(
            collective_id=0, has_side_effects=True, vmem_limit_bytes=64 * 1024 * 1024
        ),
        name="galore_step",
    )(acts, grad_out, weight, basis, first_moment, second_moment)
    direction = direction.reshape(rank, d_out)
    wide = 512
    results = (grad_in, first_new, second_new)
    blocks = [pl.BlockSpec((r.shape[0], wide), lambda j: (0, j)) for r in results]
    *results, weight_update = pl.pallas_call(
        update_kernel,
        grid=(d_out // wide,),
        out_shape=[jax.ShapeDtypeStruct(r.shape, r.dtype) for r in results]
        + [jax.ShapeDtypeStruct((basis.shape[0], d_out), BF16)],
        in_specs=[
            pl.BlockSpec(basis.shape, lambda j: (0, 0)),
            pl.BlockSpec((rank, wide), lambda j: (0, j)),
        ]
        + blocks,
        out_specs=blocks + [pl.BlockSpec((basis.shape[0], wide), lambda j: (0, j))],
        compiler_params=pltpu.CompilerParams(vmem_limit_bytes=64 * 1024 * 1024),
        name="back_projection",
    )(basis, direction, *results)
    return *results, weight_update


def on_device(acts, grad_out, weight, basis, first_moment, second_moment):
    grad_in = lax.dot_general(
        grad_out,
        lax.all_gather(weight, "fsdp", axis=0, tiled=True),
        (((1,), (1,)), ((), ())),
        preferred_element_type=F32,
    ).astype(BF16)
    coords = jnp.dot(
        acts, lax.all_gather(basis, "fsdp", axis=0, tiled=True), preferred_element_type=F32
    ).astype(BF16)
    projected = lax.psum_scatter(
        lax.dot_general(coords, grad_out, (((0,), (0,)), ((), ())), preferred_element_type=F32),
        ("dp", "fsdp"),
        scatter_dimension=0,
        tiled=True,
    )
    total = lax.psum(jnp.sum(projected * projected), ("dp", "fsdp"))
    first_new, second_new, direction = clipped_adam(
        projected, total, first_moment, second_moment, basis.shape[1] * grad_out.shape[1]
    )
    update = jnp.dot(
        basis,
        lax.all_gather(direction, ("dp", "fsdp"), axis=0, tiled=True),
        preferred_element_type=F32,
    )
    return grad_in, first_new, second_new, (0.25 * update).astype(BF16)


def solution(mesh):
    split = P(("dp", "fsdp"), None)
    halves = P("fsdp", None)
    small = mesh.shape["dp"] == 2 * PLANES and mesh.shape["fsdp"] == 2
    return jax.shard_map(
        on_device_kernel if small else on_device,
        mesh=mesh,
        in_specs=(split, split, halves, halves, split, split),
        out_specs=(split, split, split, halves),
        check_vma=False,
    )
```

```python
import functools
import math

import jax
import jax.numpy as jnp
from jax import lax
from jax.experimental import pallas as pl
from jax.experimental.pallas import tpu as pltpu
from jax.sharding import PartitionSpec as P

MESH = pl.DeviceIdType.MESH
F32 = jnp.float32
BF16 = jnp.bfloat16

first_bias = 1.0 - 0.9**10
second_bias = 1.0 - 0.999**10

PLANES = 8
DEPTH = PLANES // 2
SUBS = 2
CHUNKS = 4


def clipped_adam(projected, total, first_moment, second_moment, entries):
    limit = math.sqrt(entries)
    factor = jnp.minimum(1.0, limit / (jnp.sqrt(total) + 1e-06))
    clipped = factor * projected
    first_new = 0.9 * first_moment + 0.1 * clipped
    second_new = 0.999 * second_moment + 0.001 * clipped * clipped
    direction = first_new / first_bias / (jnp.sqrt(second_new / second_bias) + 1e-08)
    return first_new, second_new, direction.astype(BF16)


def step_kernel(
    acts_ref, grad_ref, weight_hbm, basis_hbm, first_hbm, second_hbm,
    grad_in_ref, first_out, second_out, gathered_hbm,
    weight, basis_all, acts_own, first_ref, second_ref, coords_out, grads, coords,
    feature, own, mine16, from_y, pairs, pairs16, arrived, sums_out, sums_in, gathered, back_out, back_in,
    load_sems, out_sem,
    basis_s, basis_r, coords_s, coords_r, gx_s, gx_r, gc_s, gc_r, gf_s, gf_r,
    ry_s, ry_r, rs_s, rs_r, sum_s, sum_r, back_s, back_r,
    gather_s, gather_r,
):
    dp = lax.axis_index("dp")
    x = lax.axis_index("fsdp")
    ox = 1 - x
    plane = dp // 2
    core = dp % 2
    oc = 1 - core
    me = core * 2 + x
    tokens, d_in = acts_ref.shape
    half = d_in // 2
    d_out = grad_ref.shape[1]
    wide = d_out // CHUNKS
    rank = basis_hbm.shape[1]
    piece = half // (4 * SUBS)
    quarter = rank // 4
    rows = rank // (4 * PLANES)

    def device(p, c, f):
        return {"dp": p * 2 + c, "fsdp": f}

    partner = device(plane, core, ox)
    sibling = device(plane, oc, x)
    diagonal = device(plane, oc, ox)
    z = plane // 2
    y = plane % 2
    oy = 1 - y
    beside = device(z * 2 + oy, core, x)
    planes = [device((plane + k) % PLANES, core, x) for k in range(PLANES)]
    group = [partner, sibling, diagonal]

    def send(src, dst, s, r, to):
        copy = pltpu.make_async_remote_copy(
            src_ref=src, dst_ref=dst, send_sem=s, recv_sem=r, device_id=to, device_id_type=MESH
        )
        copy.start()
        return copy

    loads = []
    for src, dst in [
        (basis_hbm, basis_all.at[x]), (acts_ref, acts_own), (grad_ref, grads.at[me]),
        (first_hbm, first_ref), (second_hbm, second_ref), (weight_hbm, weight),
    ]:
        loads.append(pltpu.make_async_copy(src, dst, load_sems.at[len(loads)]))
        loads[-1].start()
    barrier = pltpu.get_barrier_semaphore()
    for to in group + planes[1:]:
        pl.semaphore_signal(barrier, inc=1, device_id=to, device_id_type=MESH)
    pl.semaphore_wait(barrier, 2 + PLANES)

    pending = []
    basis_copies = {}

    def basis_rows(quarter_at, i):
        return pl.ds(pl.multiple_of((quarter_at * SUBS + i) * piece, piece), piece)

    def pass_basis(kind, i, src, dst, to_dev):
        basis_copies[kind, i] = send(src, dst, basis_s.at[kind, i], basis_r.at[kind, i], to_dev)

    for i in range(SUBS):
        at = basis_rows(y * 2 + core, i)
        pass_basis(0, i, basis_hbm.at[at], basis_all.at[x, at], partner)
    to_partner = []
    to_sibling = []

    def send_gradient(n):
        cols = pl.ds(n * wide, wide)
        to_partner.append(
            send(grad_ref.at[:, cols], grads.at[me, :, cols], gx_s.at[n], gx_r.at[n], partner)
        )

    send_gradient(0)
    for n in range(CHUNKS):
        cols = pl.ds(n * wide, wide)
        to_sibling.append(
            send(grad_ref.at[:, cols], grads.at[me, :, cols], gc_s.at[n], gc_r.at[n], sibling)
        )

    at = lax.broadcasted_iota(jnp.int32, (rank, rank), 0)
    to = lax.broadcasted_iota(jnp.int32, (rank, rank), 1)
    source = ((to % quarter) // rows * 4 + to // quarter) * rows + to % rows
    shuffle = jnp.where(at == source, 1.0, 0.0).astype(BF16)

    loads[0].wait()
    loads[1].wait()
    values = jnp.dot(
        acts_own[:, pl.ds(pl.multiple_of(x * half, half), half)],
        basis_all[x],
        preferred_element_type=F32,
    )
    for i in range(SUBS):
        basis_copies[0, i].wait_recv()
        at = basis_rows(y * 2 + core, i)
        block = basis_all.at[ox, at]
        pass_basis(1, i, block, block, beside)
        pass_basis(2, i, block, block, sibling)
    for n in range(1, CHUNKS):
        send_gradient(n)
    for i in range(SUBS):
        basis_copies[1, i].wait_recv()
        block = basis_all.at[ox, basis_rows(oy * 2 + core, i)]
        pass_basis(3, i, block, block, sibling)
    for kind in (2, 3):
        for i in range(SUBS):
            basis_copies[kind, i].wait_recv()
    values += jnp.dot(
        acts_own[:, pl.ds(pl.multiple_of(ox * half, half), half)],
        basis_all[ox],
        preferred_element_type=F32,
    )
    values = jnp.dot(values.astype(BF16), shuffle, preferred_element_type=F32).astype(BF16)
    for q in range(4):
        coords_out[q] = values[:, q * quarter:(q + 1) * quarter]
    coord_copies = []
    for k, (to_dev, q) in enumerate(
        [(partner, core * 2 + ox), (diagonal, oc * 2 + ox), (sibling, oc * 2 + x)]
    ):
        coord_copies.append(
            send(coords_out.at[q], coords.at[me], coords_s.at[k], coords_r.at[k], to_dev)
        )
    coords[me] = coords_out[me]
    loads[2].wait()
    for copy in coord_copies:
        copy.wait_recv()

    loads[5].wait()
    over_y = []
    scatter = []
    forward = []

    def reduce_z(n):
        cols = pl.ds(n * wide, wide)
        over_y[n].wait_recv()
        pair = own[:, y, :, cols] + from_y[:, :, cols].astype(F32)
        pairs[:, :, cols] = pair
        pairs16[:, :, cols] = pair.astype(BF16)
        for k in range(1, DEPTH):
            scatter.append(
                send(
                    pairs16.at[(z + k) % DEPTH, :, cols], arrived.at[k - 1, :, cols],
                    rs_s.at[n, k - 1], rs_r.at[n, k - 1], device((z + k) % DEPTH * 2 + y, core, x),
                )
            )

    for n in range(CHUNKS):
        cols = pl.ds(n * wide, wide)
        to_partner[n].wait_recv()
        theirs = core * 2 + ox
        forward.append(
            send(grads.at[theirs, :, cols], grads.at[theirs, :, cols], gf_s.at[n], gf_r.at[n], sibling)
        )
        to_sibling[n].wait_recv()
        forward[n].wait_recv()
        chunk = lax.dot_general(
            coords[...].reshape(4 * tokens, quarter),
            grads[:, :, cols].reshape(4 * tokens, wide),
            (((0,), (0,)), ((), ())),
            preferred_element_type=F32,
        )
        chunk = chunk.reshape(DEPTH, 2, rows, wide)
        own[:, :, :, cols] = chunk
        mine16[:, :, :, cols] = chunk.astype(BF16)
        over_y.append(
            send(
                mine16.at[:, oy, :, cols], from_y.at[:, :, cols], ry_s.at[n], ry_r.at[n], beside
            )
        )
        if n:
            reduce_z(n - 1)
        term = lax.dot_general(
            grads[pl.ds(core * 2, 2), :, cols].reshape(2 * tokens, wide),
            weight[:, cols],
            (((1,), (1,)), ((), ())),
            preferred_element_type=F32,
        ).reshape(2, tokens, half)
        if n == 0:
            feature[...] = term
        else:
            feature[...] += term

    reduce_z(CHUNKS - 1)
    back_out[...] = feature[ox].astype(BF16)
    back = send(back_out, back_in, back_s, back_r, partner)
    grad_in_ref[:, pl.ds(pl.multiple_of(x * half, half), half)] = feature[x].astype(BF16)

    loads[3].wait()
    loads[4].wait()
    for copy in scatter:
        copy.wait_recv()
    projected = pairs[z]
    for k in range(DEPTH - 1):
        projected = projected + arrived[k].astype(F32)

    sums_out[0] = jnp.full((8, 128), jnp.sum(projected * projected), F32)
    sums = []
    for k in range(1, PLANES):
        sums.append(
            send(sums_out.at[0], sums_in.at[k - 1], sum_s.at[k - 1], sum_r.at[k - 1], planes[k])
        )
    total = sums_out[0]
    for k in range(PLANES - 1):
        sums[k].wait_recv()
        total = total + sums_in[k]
    sums_out[1] = total
    for k, to_dev in enumerate(group):
        j = PLANES - 1 + k
        sums.append(send(sums_out.at[1], sums_in.at[j], sum_s.at[j], sum_r.at[j], to_dev))
    for k in range(3):
        sums[PLANES - 1 + k].wait_recv()
        total = total + sums_in[PLANES - 1 + k]
    pending += sums

    first_new, second_new, direction = clipped_adam(
        projected, total[0:1, 0:1], first_ref[...], second_ref[...], rank * d_out
    )
    gathered[plane, me] = direction
    theirs = core * 2 + ox
    left = pl.ds(0, d_out // 2)
    right = pl.ds(d_out // 2, d_out // 2)
    copies = {}

    def pass_on(kind, j, block, to_dev):
        copies[kind, j] = send(block, block, gather_s.at[kind, j], gather_r.at[kind, j], to_dev)

    for j in range(1, DEPTH):
        pass_on(0, j, gathered.at[plane, me], device((z + j) % DEPTH * 2 + y, core, x))

    def spread(j):
        if j:
            copies[0, j].wait_recv()
        block = gathered.at[(z + DEPTH - j) % DEPTH * 2 + y, me]
        pass_on(1, j, block, beside)
        pass_on(2, j, block, partner)
        pass_on(3, j, block, sibling)

    def relay(j):
        at_z = (z + DEPTH - j) % DEPTH * 2
        copies[1, j].wait_recv()
        pass_on(4, j, gathered.at[at_z + oy, me, :, left], partner)
        pass_on(5, j, gathered.at[at_z + oy, me], sibling)
        copies[2, j].wait_recv()
        pass_on(6, j, gathered.at[at_z + y, theirs, :, right], beside)
        pass_on(7, j, gathered.at[at_z + y, theirs], sibling)

    def corner(j):
        copies[4, j].wait_recv()
        copies[6, j].wait_recv()
        pass_on(8, j, gathered.at[(z + DEPTH - j) % DEPTH * 2 + oy, theirs], sibling)

    spread(0)
    first_out[...] = first_new
    second_out[...] = second_new
    for j in range(1, DEPTH + 2):
        if j < DEPTH:
            spread(j)
        if j <= DEPTH:
            relay(j - 1)
        if j >= 2:
            corner(j - 2)
    back.wait_recv()
    grad_in_ref[:, pl.ds(pl.multiple_of(ox * half, half), half)] = back_in[...]
    for kind in (3, 5, 7, 8):
        for j in range(DEPTH):
            copies[kind, j].wait_recv()
    store = pltpu.make_async_copy(gathered, gathered_hbm, out_sem)
    store.start()
    pending += [back] + list(basis_copies.values()) + to_partner + to_sibling + coord_copies + forward
    pending += over_y + scatter + list(copies.values())
    for copy in pending:
        copy.wait_send()
    store.wait()


def update_kernel(basis_ref, direction_ref, *refs):
    *results, out_ref = refs
    kept = len(results) // 2
    for src, dst in zip(results[:kept], results[kept:]):
        dst[...] = src[...]
    update = jnp.dot(basis_ref[...], direction_ref[...], preferred_element_type=F32)
    out_ref[...] = (0.25 * update).astype(BF16)


def on_device_kernel(acts, grad_out, weight, basis, first_moment, second_moment):
    tokens, d_in = acts.shape
    d_out = grad_out.shape[1]
    half = d_in // 2
    rank = basis.shape[1]
    quarter = rank // 4
    rows = rank // (4 * PLANES)
    vmem = pl.BlockSpec(memory_space=pltpu.VMEM)
    anywhere = pl.BlockSpec(memory_space=pltpu.HBM)
    dma = pltpu.SemaphoreType.DMA
    grad_in, first_new, second_new, direction = pl.pallas_call(
        step_kernel,
        out_shape=(
            jax.ShapeDtypeStruct((tokens, d_in), BF16),
            jax.ShapeDtypeStruct(first_moment.shape, F32),
            jax.ShapeDtypeStruct(second_moment.shape, F32),
            jax.ShapeDtypeStruct((PLANES, 4, rows, d_out), BF16),
        ),
        in_specs=[anywhere] * 6,
        out_specs=(vmem, vmem, vmem, pl.BlockSpec(memory_space=pl.ANY)),
        scratch_shapes=[
            pltpu.VMEM(weight.shape, BF16),
            pltpu.VMEM((2,) + basis.shape, BF16),
            pltpu.VMEM(acts.shape, BF16),
            pltpu.VMEM(first_moment.shape, F32),
            pltpu.VMEM(second_moment.shape, F32),
            pltpu.VMEM((4, tokens, quarter), BF16),
            pltpu.VMEM((4, tokens, d_out), BF16),
            pltpu.VMEM((4, tokens, quarter), BF16),
            pltpu.VMEM((2, tokens, half), F32),
            pltpu.VMEM((DEPTH, 2, rows, d_out), F32),
            pltpu.VMEM((DEPTH, 2, rows, d_out), BF16),
            pltpu.VMEM((DEPTH, rows, d_out), BF16),
            pltpu.VMEM((DEPTH, rows, d_out), F32),
            pltpu.VMEM((DEPTH, rows, d_out), BF16),
            pltpu.VMEM((DEPTH - 1, rows, d_out), BF16),
            pltpu.VMEM((2, 8, 128), F32),
            pltpu.VMEM((PLANES + 2, 8, 128), F32),
            pltpu.VMEM((PLANES, 4, rows, d_out), BF16),
            pltpu.VMEM((tokens, half), BF16),
            pltpu.VMEM((tokens, half), BF16),
            dma((6,)), dma,
            dma((4, SUBS)), dma((4, SUBS)), dma((3,)), dma((3,)),
            dma((CHUNKS,)), dma((CHUNKS,)), dma((CHUNKS,)), dma((CHUNKS,)),
            dma((CHUNKS,)), dma((CHUNKS,)),
            dma((CHUNKS,)), dma((CHUNKS,)),
            dma((CHUNKS, DEPTH - 1)), dma((CHUNKS, DEPTH - 1)),
            dma((PLANES + 2,)), dma((PLANES + 2,)), dma, dma,
            dma((9, DEPTH)), dma((9, DEPTH)),
        ],
        compiler_params=pltpu.CompilerParams(
            collective_id=0, has_side_effects=True, vmem_limit_bytes=64 * 1024 * 1024
        ),
        name="galore_step",
    )(acts, grad_out, weight, basis, first_moment, second_moment)
    direction = direction.reshape(rank, d_out)
    wide = 512
    results = (grad_in, first_new, second_new)
    blocks = [pl.BlockSpec((r.shape[0], wide), lambda j: (0, j)) for r in results]
    *results, weight_update = pl.pallas_call(
        update_kernel,
        grid=(d_out // wide,),
        out_shape=[jax.ShapeDtypeStruct(r.shape, r.dtype) for r in results]
        + [jax.ShapeDtypeStruct((basis.shape[0], d_out), BF16)],
        in_specs=[
            pl.BlockSpec(basis.shape, lambda j: (0, 0)),
            pl.BlockSpec((rank, wide), lambda j: (0, j)),
        ]
        + blocks,
        out_specs=blocks + [pl.BlockSpec((basis.shape[0], wide), lambda j: (0, j))],
        compiler_params=pltpu.CompilerParams(vmem_limit_bytes=64 * 1024 * 1024),
        name="back_projection",
    )(basis, direction, *results)
    return *results, weight_update


def on_device(acts, grad_out, weight, basis, first_moment, second_moment):
    grad_in = lax.dot_general(
        grad_out,
        lax.all_gather(weight, "fsdp", axis=0, tiled=True),
        (((1,), (1,)), ((), ())),
        preferred_element_type=F32,
    ).astype(BF16)
    coords = jnp.dot(
        acts, lax.all_gather(basis, "fsdp", axis=0, tiled=True), preferred_element_type=F32
    ).astype(BF16)
    projected = lax.psum_scatter(
        lax.dot_general(coords, grad_out, (((0,), (0,)), ((), ())), preferred_element_type=F32),
        ("dp", "fsdp"),
        scatter_dimension=0,
        tiled=True,
    )
    total = lax.psum(jnp.sum(projected * projected), ("dp", "fsdp"))
    first_new, second_new, direction = clipped_adam(
        projected, total, first_moment, second_moment, basis.shape[1] * grad_out.shape[1]
    )
    update = jnp.dot(
        basis,
        lax.all_gather(direction, ("dp", "fsdp"), axis=0, tiled=True),
        preferred_element_type=F32,
    )
    return grad_in, first_new, second_new, (0.25 * update).astype(BF16)


def solution(mesh):
    split = P(("dp", "fsdp"), None)
    halves = P("fsdp", None)
    small = mesh.shape["dp"] == 2 * PLANES and mesh.shape["fsdp"] == 2
    return jax.shard_map(
        on_device_kernel if small else on_device,
        mesh=mesh,
        in_specs=(split, split, halves, halves, split, split),
        out_specs=(split, split, split, halves),
        check_vma=False,
    )
```

```python
import functools
import math

import jax
import jax.numpy as jnp
from jax import lax
from jax.experimental import pallas as pl
from jax.experimental.pallas import tpu as pltpu
from jax.sharding import PartitionSpec as P

MESH = pl.DeviceIdType.MESH
F32 = jnp.float32
BF16 = jnp.bfloat16

first_bias = 1.0 - 0.9**10
second_bias = 1.0 - 0.999**10

PLANES = 8
DEPTH = PLANES // 2
CHUNKS = 4


def clipped_adam(projected, total, first_moment, second_moment, entries):
    limit = math.sqrt(entries)
    factor = jnp.minimum(1.0, limit / (jnp.sqrt(total) + 1e-06))
    clipped = factor * projected
    first_new = 0.9 * first_moment + 0.1 * clipped
    second_new = 0.999 * second_moment + 0.001 * clipped * clipped
    direction = first_new / first_bias / (jnp.sqrt(second_new / second_bias) + 1e-08)
    return first_new, second_new, direction.astype(BF16)


def step_kernel(
    acts_ref, grad_ref, weight_hbm, basis_hbm, first_hbm, second_hbm,
    grad_in_ref, first_out, second_out, gathered_hbm,
    weight, basis_ref, first_ref, second_ref, acts_pair, basis_perm, partial, partial_in, grads, coords,
    feature, own, mine16, from_y, pairs, pairs16, arrived, sums_out, sums_in, gathered, back_out, back_in,
    load_sems, out_sem,
    acts_s, acts_r, coords_s, coords_r, gx_s, gx_r, gc_s, gc_r, gf_s, gf_r,
    ry_s, ry_r, rs_s, rs_r, sum_s, sum_r, back_s, back_r,
    gather_s, gather_r,
):
    dp = lax.axis_index("dp")
    x = lax.axis_index("fsdp")
    ox = 1 - x
    plane = dp // 2
    core = dp % 2
    oc = 1 - core
    me = core * 2 + x
    tokens, d_in = acts_ref.shape
    half = d_in // 2
    d_out = grad_ref.shape[1]
    wide = d_out // CHUNKS
    rank = basis_ref.shape[1]
    quarter = rank // 4
    rows = rank // (4 * PLANES)

    def device(p, c, f):
        return {"dp": p * 2 + c, "fsdp": f}

    partner = device(plane, core, ox)
    sibling = device(plane, oc, x)
    diagonal = device(plane, oc, ox)
    planes = [device((plane + k) % PLANES, core, x) for k in range(PLANES)]
    group = [partner, sibling, diagonal]

    def send(src, dst, s, r, to):
        copy = pltpu.make_async_remote_copy(
            src_ref=src, dst_ref=dst, send_sem=s, recv_sem=r, device_id=to, device_id_type=MESH
        )
        copy.start()
        return copy

    loads = []
    own_half = acts_ref.at[:, pl.ds(pl.multiple_of(x * half, half), half)]
    for src, dst in [
        (basis_hbm, basis_ref), (own_half, acts_pair.at[x]), (grad_ref, grads.at[me]),
        (first_hbm, first_ref), (second_hbm, second_ref), (weight_hbm, weight),
    ]:
        loads.append(pltpu.make_async_copy(src, dst, load_sems.at[len(loads)]))
        loads[-1].start()
    barrier = pltpu.get_barrier_semaphore()
    for to in group + planes[1:]:
        pl.semaphore_signal(barrier, inc=1, device_id=to, device_id_type=MESH)
    pl.semaphore_wait(barrier, 2 + PLANES)

    pending = []
    acts_copy = send(
        acts_ref.at[:, pl.ds(pl.multiple_of(ox * half, half), half)],
        acts_pair.at[x], acts_s, acts_r, partner,
    )
    to_partner = []
    to_sibling = []

    def send_gradient(n):
        cols = pl.ds(n * wide, wide)
        to_partner.append(
            send(grad_ref.at[:, cols], grads.at[me, :, cols], gx_s.at[n], gx_r.at[n], partner)
        )

    send_gradient(0)
    for n in range(CHUNKS):
        cols = pl.ds(n * wide, wide)
        to_sibling.append(
            send(grad_ref.at[:, cols], grads.at[me, :, cols], gc_s.at[n], gc_r.at[n], sibling)
        )

    at = lax.broadcasted_iota(jnp.int32, (rank, rank), 0)
    to = lax.broadcasted_iota(jnp.int32, (rank, rank), 1)
    source = ((to % quarter) // rows * 4 + to // quarter) * rows + to % rows
    shuffle = jnp.where(at == source, 1.0, 0.0).astype(BF16)
    loads[0].wait()
    basis_perm[...] = jnp.dot(basis_ref[...], shuffle, preferred_element_type=F32).astype(BF16)

    def project(block):
        return jnp.dot(block, basis_perm[...], preferred_element_type=F32)

    loads[1].wait()
    values = project(acts_pair[x])
    for q in range(4):
        partial[q, x] = values[:, q * quarter:(q + 1) * quarter]
    acts_copy.wait_recv()
    values = project(acts_pair[ox])
    for q in range(4):
        partial[q, ox] = values[:, q * quarter:(q + 1) * quarter]
    coord_copies = []
    for k, (to_dev, q) in enumerate(
        [(partner, core * 2 + ox), (diagonal, oc * 2 + ox), (sibling, oc * 2 + x)]
    ):
        coord_copies.append(
            send(partial.at[q], partial_in.at[k], coords_s.at[k], coords_r.at[k], to_dev)
        )
    for n in range(1, CHUNKS):
        send_gradient(n)
    loads[2].wait()
    for copy in coord_copies:
        copy.wait_recv()
    coords[core] = (partial[me] + partial_in[0]).astype(BF16)
    coords[oc] = (partial_in[1] + partial_in[2]).astype(BF16)

    loads[5].wait()
    z = plane // 2
    y = plane % 2
    oy = 1 - y
    beside = device(z * 2 + oy, core, x)
    over_y = []
    scatter = []
    forward = []

    def reduce_z(n):
        cols = pl.ds(n * wide, wide)
        over_y[n].wait_recv()
        pair = own[:, y, :, cols] + from_y[:, :, cols].astype(F32)
        pairs[:, :, cols] = pair
        pairs16[:, :, cols] = pair.astype(BF16)
        for k in range(1, DEPTH):
            scatter.append(
                send(
                    pairs16.at[(z + k) % DEPTH, :, cols], arrived.at[k - 1, :, cols],
                    rs_s.at[n, k - 1], rs_r.at[n, k - 1], device((z + k) % DEPTH * 2 + y, core, x),
                )
            )

    for n in range(CHUNKS):
        cols = pl.ds(n * wide, wide)
        to_partner[n].wait_recv()
        theirs = core * 2 + ox
        forward.append(
            send(grads.at[theirs, :, cols], grads.at[theirs, :, cols], gf_s.at[n], gf_r.at[n], sibling)
        )
        to_sibling[n].wait_recv()
        forward[n].wait_recv()
        chunk = lax.dot_general(
            coords[...].reshape(4 * tokens, quarter),
            grads[:, :, cols].reshape(4 * tokens, wide),
            (((0,), (0,)), ((), ())),
            preferred_element_type=F32,
        )
        chunk = chunk.reshape(DEPTH, 2, rows, wide)
        own[:, :, :, cols] = chunk
        mine16[:, :, :, cols] = chunk.astype(BF16)
        over_y.append(
            send(
                mine16.at[:, oy, :, cols], from_y.at[:, :, cols], ry_s.at[n], ry_r.at[n], beside
            )
        )
        if n:
            reduce_z(n - 1)
        term = lax.dot_general(
            grads[pl.ds(core * 2, 2), :, cols].reshape(2 * tokens, wide),
            weight[:, cols],
            (((1,), (1,)), ((), ())),
            preferred_element_type=F32,
        ).reshape(2, tokens, half)
        if n == 0:
            feature[...] = term
        else:
            feature[...] += term

    reduce_z(CHUNKS - 1)
    back_out[...] = feature[ox].astype(BF16)
    back = send(back_out, back_in, back_s, back_r, partner)
    grad_in_ref[:, pl.ds(pl.multiple_of(x * half, half), half)] = feature[x].astype(BF16)

    loads[3].wait()
    loads[4].wait()
    for copy in scatter:
        copy.wait_recv()
    projected = pairs[z]
    for k in range(DEPTH - 1):
        projected = projected + arrived[k].astype(F32)

    sums_out[0] = jnp.full((8, 128), jnp.sum(projected * projected), F32)
    sums = []
    for k in range(1, PLANES):
        sums.append(
            send(sums_out.at[0], sums_in.at[k - 1], sum_s.at[k - 1], sum_r.at[k - 1], planes[k])
        )
    total = sums_out[0]
    for k in range(PLANES - 1):
        sums[k].wait_recv()
        total = total + sums_in[k]
    sums_out[1] = total
    for k, to_dev in enumerate(group):
        j = PLANES - 1 + k
        sums.append(send(sums_out.at[1], sums_in.at[j], sum_s.at[j], sum_r.at[j], to_dev))
    for k in range(3):
        sums[PLANES - 1 + k].wait_recv()
        total = total + sums_in[PLANES - 1 + k]
    pending += sums

    first_new, second_new, direction = clipped_adam(
        projected, total[0:1, 0:1], first_ref[...], second_ref[...], rank * d_out
    )
    gathered[plane, me] = direction
    theirs = core * 2 + ox
    left = pl.ds(0, d_out // 2)
    right = pl.ds(d_out // 2, d_out // 2)
    copies = {}

    def pass_on(kind, j, block, to_dev):
        copies[kind, j] = send(block, block, gather_s.at[kind, j], gather_r.at[kind, j], to_dev)

    for j in range(1, DEPTH):
        pass_on(0, j, gathered.at[plane, me], device((z + j) % DEPTH * 2 + y, core, x))

    def spread(j):
        if j:
            copies[0, j].wait_recv()
        block = gathered.at[(z + DEPTH - j) % DEPTH * 2 + y, me]
        pass_on(1, j, block, beside)
        pass_on(2, j, block, partner)
        pass_on(3, j, block, sibling)

    def relay(j):
        at_z = (z + DEPTH - j) % DEPTH * 2
        copies[1, j].wait_recv()
        pass_on(4, j, gathered.at[at_z + oy, me, :, left], partner)
        pass_on(5, j, gathered.at[at_z + oy, me], sibling)
        copies[2, j].wait_recv()
        pass_on(6, j, gathered.at[at_z + y, theirs, :, right], beside)
        pass_on(7, j, gathered.at[at_z + y, theirs], sibling)

    def corner(j):
        copies[4, j].wait_recv()
        copies[6, j].wait_recv()
        pass_on(8, j, gathered.at[(z + DEPTH - j) % DEPTH * 2 + oy, theirs], sibling)

    spread(0)
    first_out[...] = first_new
    second_out[...] = second_new
    for j in range(1, DEPTH + 2):
        if j < DEPTH:
            spread(j)
        if j <= DEPTH:
            relay(j - 1)
        if j >= 2:
            corner(j - 2)
    back.wait_recv()
    grad_in_ref[:, pl.ds(pl.multiple_of(ox * half, half), half)] = back_in[...]
    for kind in (3, 5, 7, 8):
        for j in range(DEPTH):
            copies[kind, j].wait_recv()
    store = pltpu.make_async_copy(gathered, gathered_hbm, out_sem)
    store.start()
    pending += [acts_copy, back] + to_partner + to_sibling + coord_copies + forward
    pending += over_y + scatter + list(copies.values())
    for copy in pending:
        copy.wait_send()
    store.wait()


def update_kernel(basis_ref, direction_ref, *refs):
    *results, out_ref = refs
    kept = len(results) // 2
    for src, dst in zip(results[:kept], results[kept:]):
        dst[...] = src[...]
    update = jnp.dot(basis_ref[...], direction_ref[...], preferred_element_type=F32)
    out_ref[...] = (0.25 * update).astype(BF16)


def on_device_kernel(acts, grad_out, weight, basis, first_moment, second_moment):
    tokens, d_in = acts.shape
    d_out = grad_out.shape[1]
    half = d_in // 2
    rank = basis.shape[1]
    quarter = rank // 4
    rows = rank // (4 * PLANES)
    vmem = pl.BlockSpec(memory_space=pltpu.VMEM)
    anywhere = pl.BlockSpec(memory_space=pltpu.HBM)
    dma = pltpu.SemaphoreType.DMA
    grad_in, first_new, second_new, direction = pl.pallas_call(
        step_kernel,
        out_shape=(
            jax.ShapeDtypeStruct((tokens, d_in), BF16),
            jax.ShapeDtypeStruct(first_moment.shape, F32),
            jax.ShapeDtypeStruct(second_moment.shape, F32),
            jax.ShapeDtypeStruct((PLANES, 4, rows, d_out), BF16),
        ),
        in_specs=[anywhere] * 6,
        out_specs=(vmem, vmem, vmem, pl.BlockSpec(memory_space=pl.ANY)),
        scratch_shapes=[
            pltpu.VMEM(weight.shape, BF16),
            pltpu.VMEM(basis.shape, BF16),
            pltpu.VMEM(first_moment.shape, F32),
            pltpu.VMEM(second_moment.shape, F32),
            pltpu.VMEM((2, tokens, half), BF16),
            pltpu.VMEM(basis.shape, BF16),
            pltpu.VMEM((4, 2, tokens, quarter), F32),
            pltpu.VMEM((3, 2, tokens, quarter), F32),
            pltpu.VMEM((4, tokens, d_out), BF16),
            pltpu.VMEM((2, 2, tokens, quarter), BF16),
            pltpu.VMEM((2, tokens, half), F32),
            pltpu.VMEM((DEPTH, 2, rows, d_out), F32),
            pltpu.VMEM((DEPTH, 2, rows, d_out), BF16),
            pltpu.VMEM((DEPTH, rows, d_out), BF16),
            pltpu.VMEM((DEPTH, rows, d_out), F32),
            pltpu.VMEM((DEPTH, rows, d_out), BF16),
            pltpu.VMEM((DEPTH - 1, rows, d_out), BF16),
            pltpu.VMEM((2, 8, 128), F32),
            pltpu.VMEM((PLANES + 2, 8, 128), F32),
            pltpu.VMEM((PLANES, 4, rows, d_out), BF16),
            pltpu.VMEM((tokens, half), BF16),
            pltpu.VMEM((tokens, half), BF16),
            dma((6,)), dma,
            dma, dma, dma((3,)), dma((3,)),
            dma((CHUNKS,)), dma((CHUNKS,)), dma((CHUNKS,)), dma((CHUNKS,)),
            dma((CHUNKS,)), dma((CHUNKS,)),
            dma((CHUNKS,)), dma((CHUNKS,)),
            dma((CHUNKS, DEPTH - 1)), dma((CHUNKS, DEPTH - 1)),
            dma((PLANES + 2,)), dma((PLANES + 2,)), dma, dma,
            dma((9, DEPTH)), dma((9, DEPTH)),
        ],
        compiler_params=pltpu.CompilerParams(
            collective_id=0, has_side_effects=True, vmem_limit_bytes=64 * 1024 * 1024
        ),
        name="galore_step",
    )(acts, grad_out, weight, basis, first_moment, second_moment)
    direction = direction.reshape(rank, d_out)
    wide = 512
    results = (grad_in, first_new, second_new)
    blocks = [pl.BlockSpec((r.shape[0], wide), lambda j: (0, j)) for r in results]
    *results, weight_update = pl.pallas_call(
        update_kernel,
        grid=(d_out // wide,),
        out_shape=[jax.ShapeDtypeStruct(r.shape, r.dtype) for r in results]
        + [jax.ShapeDtypeStruct((basis.shape[0], d_out), BF16)],
        in_specs=[
            pl.BlockSpec(basis.shape, lambda j: (0, 0)),
            pl.BlockSpec((rank, wide), lambda j: (0, j)),
        ]
        + blocks,
        out_specs=blocks + [pl.BlockSpec((basis.shape[0], wide), lambda j: (0, j))],
        compiler_params=pltpu.CompilerParams(vmem_limit_bytes=64 * 1024 * 1024),
        name="back_projection",
    )(basis, direction, *results)
    return *results, weight_update


def on_device(acts, grad_out, weight, basis, first_moment, second_moment):
    grad_in = lax.dot_general(
        grad_out,
        lax.all_gather(weight, "fsdp", axis=0, tiled=True),
        (((1,), (1,)), ((), ())),
        preferred_element_type=F32,
    ).astype(BF16)
    coords = jnp.dot(
        acts, lax.all_gather(basis, "fsdp", axis=0, tiled=True), preferred_element_type=F32
    ).astype(BF16)
    projected = lax.psum_scatter(
        lax.dot_general(coords, grad_out, (((0,), (0,)), ((), ())), preferred_element_type=F32),
        ("dp", "fsdp"),
        scatter_dimension=0,
        tiled=True,
    )
    total = lax.psum(jnp.sum(projected * projected), ("dp", "fsdp"))
    first_new, second_new, direction = clipped_adam(
        projected, total, first_moment, second_moment, basis.shape[1] * grad_out.shape[1]
    )
    update = jnp.dot(
        basis,
        lax.all_gather(direction, ("dp", "fsdp"), axis=0, tiled=True),
        preferred_element_type=F32,
    )
    return grad_in, first_new, second_new, (0.25 * update).astype(BF16)


def solution(mesh):
    split = P(("dp", "fsdp"), None)
    halves = P("fsdp", None)
    small = mesh.shape["dp"] == 2 * PLANES and mesh.shape["fsdp"] == 2
    return jax.shard_map(
        on_device_kernel if small else on_device,
        mesh=mesh,
        in_specs=(split, split, halves, halves, split, split),
        out_specs=(split, split, split, halves),
        check_vma=False,
    )
```

```python
import functools
import math

import jax
import jax.numpy as jnp
from jax import lax
from jax.experimental import pallas as pl
from jax.experimental.pallas import tpu as pltpu
from jax.sharding import PartitionSpec as P

MESH = pl.DeviceIdType.MESH
F32 = jnp.float32
BF16 = jnp.bfloat16

first_bias = 1.0 - 0.9**10
second_bias = 1.0 - 0.999**10

PLANES = 8
DEPTH = PLANES // 2
CHUNKS = 2


def clipped_adam(projected, total, first_moment, second_moment, entries):
    limit = math.sqrt(entries)
    factor = jnp.minimum(1.0, limit / (jnp.sqrt(total) + 1e-06))
    clipped = factor * projected
    first_new = 0.9 * first_moment + 0.1 * clipped
    second_new = 0.999 * second_moment + 0.001 * clipped * clipped
    direction = first_new / first_bias / (jnp.sqrt(second_new / second_bias) + 1e-08)
    return first_new, second_new, direction.astype(BF16)


def step_kernel(
    acts_ref, grad_ref, weight_hbm, basis_hbm, first_hbm, second_hbm,
    grad_in_ref, first_out, second_out, gathered_hbm,
    weight, basis_ref, first_ref, second_ref, acts_pair, basis_perm, partial, partial_in, grads, coords,
    feature, own, mine16, arrived, sums_out, sums_in, gathered, back_out, back_in,
    load_sems, out_sem,
    acts_s, acts_r, coords_s, coords_r, gx_s, gx_r, gc_s, gc_r, gf_s, gf_r,
    rs_s, rs_r, sum_s, sum_r, back_s, back_r,
    gather_s, gather_r,
):
    dp = lax.axis_index("dp")
    x = lax.axis_index("fsdp")
    ox = 1 - x
    plane = dp // 2
    core = dp % 2
    oc = 1 - core
    me = core * 2 + x
    tokens, d_in = acts_ref.shape
    half = d_in // 2
    d_out = grad_ref.shape[1]
    wide = d_out // CHUNKS
    rank = basis_ref.shape[1]
    quarter = rank // 4
    rows = rank // (4 * PLANES)

    def device(p, c, f):
        return {"dp": p * 2 + c, "fsdp": f}

    partner = device(plane, core, ox)
    sibling = device(plane, oc, x)
    diagonal = device(plane, oc, ox)
    planes = [device((plane + k) % PLANES, core, x) for k in range(PLANES)]
    group = [partner, sibling, diagonal]

    def send(src, dst, s, r, to):
        copy = pltpu.make_async_remote_copy(
            src_ref=src, dst_ref=dst, send_sem=s, recv_sem=r, device_id=to, device_id_type=MESH
        )
        copy.start()
        return copy

    loads = []
    own_half = acts_ref.at[:, pl.ds(pl.multiple_of(x * half, half), half)]
    for src, dst in [
        (basis_hbm, basis_ref), (own_half, acts_pair.at[x]), (grad_ref, grads.at[me]),
        (first_hbm, first_ref), (second_hbm, second_ref), (weight_hbm, weight),
    ]:
        loads.append(pltpu.make_async_copy(src, dst, load_sems.at[len(loads)]))
        loads[-1].start()
    barrier = pltpu.get_barrier_semaphore()
    for to in group + planes[1:]:
        pl.semaphore_signal(barrier, inc=1, device_id=to, device_id_type=MESH)
    pl.semaphore_wait(barrier, 2 + PLANES)

    pending = []
    acts_copy = send(
        acts_ref.at[:, pl.ds(pl.multiple_of(ox * half, half), half)],
        acts_pair.at[x], acts_s, acts_r, partner,
    )
    to_partner = []
    to_sibling = []

    def send_gradient(n):
        cols = pl.ds(n * wide, wide)
        to_partner.append(
            send(grad_ref.at[:, cols], grads.at[me, :, cols], gx_s.at[n], gx_r.at[n], partner)
        )

    send_gradient(0)
    for n in range(CHUNKS):
        cols = pl.ds(n * wide, wide)
        to_sibling.append(
            send(grad_ref.at[:, cols], grads.at[me, :, cols], gc_s.at[n], gc_r.at[n], sibling)
        )

    at = lax.broadcasted_iota(jnp.int32, (rank, rank), 0)
    to = lax.broadcasted_iota(jnp.int32, (rank, rank), 1)
    source = ((to % quarter) // rows * 4 + to // quarter) * rows + to % rows
    shuffle = jnp.where(at == source, 1.0, 0.0).astype(BF16)
    loads[0].wait()
    basis_perm[...] = jnp.dot(basis_ref[...], shuffle, preferred_element_type=F32).astype(BF16)

    def project(block):
        return jnp.dot(block, basis_perm[...], preferred_element_type=F32)

    loads[1].wait()
    values = project(acts_pair[x])
    for q in range(4):
        partial[q, x] = values[:, q * quarter:(q + 1) * quarter]
    acts_copy.wait_recv()
    values = project(acts_pair[ox])
    for q in range(4):
        partial[q, ox] = values[:, q * quarter:(q + 1) * quarter]
    coord_copies = []
    for k, (to_dev, q) in enumerate(
        [(partner, core * 2 + ox), (diagonal, oc * 2 + ox), (sibling, oc * 2 + x)]
    ):
        coord_copies.append(
            send(partial.at[q], partial_in.at[k], coords_s.at[k], coords_r.at[k], to_dev)
        )
    for n in range(1, CHUNKS):
        send_gradient(n)
    loads[2].wait()
    for copy in coord_copies:
        copy.wait_recv()
    coords[core] = (partial[me] + partial_in[0]).astype(BF16)
    coords[oc] = (partial_in[1] + partial_in[2]).astype(BF16)

    loads[5].wait()
    scatter = []
    forward = []
    for n in range(CHUNKS):
        cols = pl.ds(n * wide, wide)
        to_partner[n].wait_recv()
        theirs = core * 2 + ox
        forward.append(
            send(grads.at[theirs, :, cols], grads.at[theirs, :, cols], gf_s.at[n], gf_r.at[n], sibling)
        )
        to_sibling[n].wait_recv()
        forward[n].wait_recv()
        chunk = lax.dot_general(
            coords[...].reshape(4 * tokens, quarter),
            grads[:, :, cols].reshape(4 * tokens, wide),
            (((0,), (0,)), ((), ())),
            preferred_element_type=F32,
        )
        chunk = chunk.reshape(PLANES, rows, wide)
        own[:, :, cols] = chunk
        mine16[:, :, cols] = chunk.astype(BF16)
        for k in range(1, PLANES):
            scatter.append(
                send(
                    mine16.at[(plane + k) % PLANES, :, cols], arrived.at[k - 1, :, cols],
                    rs_s.at[n, k - 1], rs_r.at[n, k - 1], planes[k],
                )
            )
        term = lax.dot_general(
            grads[pl.ds(core * 2, 2), :, cols].reshape(2 * tokens, wide),
            weight[:, cols],
            (((1,), (1,)), ((), ())),
            preferred_element_type=F32,
        ).reshape(2, tokens, half)
        if n == 0:
            feature[...] = term
        else:
            feature[...] += term

    back_out[...] = feature[ox].astype(BF16)
    back = send(back_out, back_in, back_s, back_r, partner)
    grad_in_ref[:, pl.ds(pl.multiple_of(x * half, half), half)] = feature[x].astype(BF16)

    loads[3].wait()
    loads[4].wait()
    for copy in scatter:
        copy.wait_recv()
    projected = own[plane]
    for k in range(PLANES - 1):
        projected = projected + arrived[k].astype(F32)

    sums_out[0] = jnp.full((8, 128), jnp.sum(projected * projected), F32)
    sums = []
    for k in range(1, PLANES):
        sums.append(
            send(sums_out.at[0], sums_in.at[k - 1], sum_s.at[k - 1], sum_r.at[k - 1], planes[k])
        )
    total = sums_out[0]
    for k in range(PLANES - 1):
        sums[k].wait_recv()
        total = total + sums_in[k]
    sums_out[1] = total
    for k, to_dev in enumerate(group):
        j = PLANES - 1 + k
        sums.append(send(sums_out.at[1], sums_in.at[j], sum_s.at[j], sum_r.at[j], to_dev))
    for k in range(3):
        sums[PLANES - 1 + k].wait_recv()
        total = total + sums_in[PLANES - 1 + k]
    pending += sums

    first_new, second_new, direction = clipped_adam(
        projected, total[0:1, 0:1], first_ref[...], second_ref[...], rank * d_out
    )
    gathered[plane, me] = direction
    z = plane // 2
    y = plane % 2
    oy = 1 - y
    theirs = core * 2 + ox
    beside = device(z * 2 + oy, core, x)
    left = pl.ds(0, d_out // 2)
    right = pl.ds(d_out // 2, d_out // 2)
    copies = {}

    def pass_on(kind, j, block, to_dev):
        copies[kind, j] = send(block, block, gather_s.at[kind, j], gather_r.at[kind, j], to_dev)

    for j in range(1, DEPTH):
        pass_on(0, j, gathered.at[plane, me], device((z + j) % DEPTH * 2 + y, core, x))

    def spread(j):
        if j:
            copies[0, j].wait_recv()
        block = gathered.at[(z + DEPTH - j) % DEPTH * 2 + y, me]
        pass_on(1, j, block, beside)
        pass_on(2, j, block, partner)
        pass_on(3, j, block, sibling)

    def relay(j):
        at_z = (z + DEPTH - j) % DEPTH * 2
        copies[1, j].wait_recv()
        pass_on(4, j, gathered.at[at_z + oy, me, :, left], partner)
        pass_on(5, j, gathered.at[at_z + oy, me], sibling)
        copies[2, j].wait_recv()
        pass_on(6, j, gathered.at[at_z + y, theirs, :, right], beside)
        pass_on(7, j, gathered.at[at_z + y, theirs], sibling)

    def corner(j):
        copies[4, j].wait_recv()
        copies[6, j].wait_recv()
        pass_on(8, j, gathered.at[(z + DEPTH - j) % DEPTH * 2 + oy, theirs], sibling)

    spread(0)
    first_out[...] = first_new
    second_out[...] = second_new
    for j in range(1, DEPTH + 2):
        if j < DEPTH:
            spread(j)
        if j <= DEPTH:
            relay(j - 1)
        if j >= 2:
            corner(j - 2)
    back.wait_recv()
    grad_in_ref[:, pl.ds(pl.multiple_of(ox * half, half), half)] = back_in[...]
    for kind in (3, 5, 7, 8):
        for j in range(DEPTH):
            copies[kind, j].wait_recv()
    store = pltpu.make_async_copy(gathered, gathered_hbm, out_sem)
    store.start()
    pending += [acts_copy, back] + to_partner + to_sibling + coord_copies + forward
    pending += scatter + list(copies.values())
    for copy in pending:
        copy.wait_send()
    store.wait()


def update_kernel(basis_ref, direction_ref, *refs):
    *results, out_ref = refs
    kept = len(results) // 2
    for src, dst in zip(results[:kept], results[kept:]):
        dst[...] = src[...]
    update = jnp.dot(basis_ref[...], direction_ref[...], preferred_element_type=F32)
    out_ref[...] = (0.25 * update).astype(BF16)


def on_device_kernel(acts, grad_out, weight, basis, first_moment, second_moment):
    tokens, d_in = acts.shape
    d_out = grad_out.shape[1]
    half = d_in // 2
    rank = basis.shape[1]
    quarter = rank // 4
    rows = rank // (4 * PLANES)
    vmem = pl.BlockSpec(memory_space=pltpu.VMEM)
    anywhere = pl.BlockSpec(memory_space=pltpu.HBM)
    dma = pltpu.SemaphoreType.DMA
    grad_in, first_new, second_new, direction = pl.pallas_call(
        step_kernel,
        out_shape=(
            jax.ShapeDtypeStruct((tokens, d_in), BF16),
            jax.ShapeDtypeStruct(first_moment.shape, F32),
            jax.ShapeDtypeStruct(second_moment.shape, F32),
            jax.ShapeDtypeStruct((PLANES, 4, rows, d_out), BF16),
        ),
        in_specs=[anywhere] * 6,
        out_specs=(vmem, vmem, vmem, pl.BlockSpec(memory_space=pl.ANY)),
        scratch_shapes=[
            pltpu.VMEM(weight.shape, BF16),
            pltpu.VMEM(basis.shape, BF16),
            pltpu.VMEM(first_moment.shape, F32),
            pltpu.VMEM(second_moment.shape, F32),
            pltpu.VMEM((2, tokens, half), BF16),
            pltpu.VMEM(basis.shape, BF16),
            pltpu.VMEM((4, 2, tokens, quarter), F32),
            pltpu.VMEM((3, 2, tokens, quarter), F32),
            pltpu.VMEM((4, tokens, d_out), BF16),
            pltpu.VMEM((2, 2, tokens, quarter), BF16),
            pltpu.VMEM((2, tokens, half), F32),
            pltpu.VMEM((PLANES, rows, d_out), F32),
            pltpu.VMEM((PLANES, rows, d_out), BF16),
            pltpu.VMEM((PLANES - 1, rows, d_out), BF16),
            pltpu.VMEM((2, 8, 128), F32),
            pltpu.VMEM((PLANES + 2, 8, 128), F32),
            pltpu.VMEM((PLANES, 4, rows, d_out), BF16),
            pltpu.VMEM((tokens, half), BF16),
            pltpu.VMEM((tokens, half), BF16),
            dma((6,)), dma,
            dma, dma, dma((3,)), dma((3,)),
            dma((CHUNKS,)), dma((CHUNKS,)), dma((CHUNKS,)), dma((CHUNKS,)),
            dma((CHUNKS,)), dma((CHUNKS,)),
            dma((CHUNKS, PLANES - 1)), dma((CHUNKS, PLANES - 1)),
            dma((PLANES + 2,)), dma((PLANES + 2,)), dma, dma,
            dma((9, DEPTH)), dma((9, DEPTH)),
        ],
        compiler_params=pltpu.CompilerParams(
            collective_id=0, has_side_effects=True, vmem_limit_bytes=64 * 1024 * 1024
        ),
        name="galore_step",
    )(acts, grad_out, weight, basis, first_moment, second_moment)
    direction = direction.reshape(rank, d_out)
    wide = 512
    results = (grad_in, first_new, second_new)
    blocks = [pl.BlockSpec((r.shape[0], wide), lambda j: (0, j)) for r in results]
    *results, weight_update = pl.pallas_call(
        update_kernel,
        grid=(d_out // wide,),
        out_shape=[jax.ShapeDtypeStruct(r.shape, r.dtype) for r in results]
        + [jax.ShapeDtypeStruct((basis.shape[0], d_out), BF16)],
        in_specs=[
            pl.BlockSpec(basis.shape, lambda j: (0, 0)),
            pl.BlockSpec((rank, wide), lambda j: (0, j)),
        ]
        + blocks,
        out_specs=blocks + [pl.BlockSpec((basis.shape[0], wide), lambda j: (0, j))],
        compiler_params=pltpu.CompilerParams(vmem_limit_bytes=64 * 1024 * 1024),
        name="back_projection",
    )(basis, direction, *results)
    return *results, weight_update


def on_device(acts, grad_out, weight, basis, first_moment, second_moment):
    grad_in = lax.dot_general(
        grad_out,
        lax.all_gather(weight, "fsdp", axis=0, tiled=True),
        (((1,), (1,)), ((), ())),
        preferred_element_type=F32,
    ).astype(BF16)
    coords = jnp.dot(
        acts, lax.all_gather(basis, "fsdp", axis=0, tiled=True), preferred_element_type=F32
    ).astype(BF16)
    projected = lax.psum_scatter(
        lax.dot_general(coords, grad_out, (((0,), (0,)), ((), ())), preferred_element_type=F32),
        ("dp", "fsdp"),
        scatter_dimension=0,
        tiled=True,
    )
    total = lax.psum(jnp.sum(projected * projected), ("dp", "fsdp"))
    first_new, second_new, direction = clipped_adam(
        projected, total, first_moment, second_moment, basis.shape[1] * grad_out.shape[1]
    )
    update = jnp.dot(
        basis,
        lax.all_gather(direction, ("dp", "fsdp"), axis=0, tiled=True),
        preferred_element_type=F32,
    )
    return grad_in, first_new, second_new, (0.25 * update).astype(BF16)


def solution(mesh):
    split = P(("dp", "fsdp"), None)
    halves = P("fsdp", None)
    small = mesh.shape["dp"] == 2 * PLANES and mesh.shape["fsdp"] == 2
    return jax.shard_map(
        on_device_kernel if small else on_device,
        mesh=mesh,
        in_specs=(split, split, halves, halves, split, split),
        out_specs=(split, split, split, halves),
        check_vma=False,
    )
```
